512 devices in a mesh: mode: 16 (over x_hi, y, core), space: 32 (over x_lo, z).
Axes of the slice: x: 4 (x_hi: 2, x_lo: 2; x = x_hi * 2 + x_lo), y: 4, z: 16, core: 2. Of those that a mesh axis runs over, the one named last changes fastest.
Arguments:
- residual: float32 [32, 2, 512, 128], P('mode', None, 'space'), may hold values from -6 to 6
- solution: float32 [32, 2, 512, 128], P('mode', None, 'space'), may hold values from -6 to 6
- kl_terms: float32 [21, 2, 512, 128], P(None, None, 'space'), may hold values from -2.5 to 4, as said below
- partner: int32 [32, 24], P('mode'), may hold values from 0 to 31
- kl_index: int32 [32, 24], P('mode'), may hold values from 1 to 20
- coefficient: float32 [32, 24], P('mode'), may hold values from -4 to 4
Outputs:
- image: float32 [32, 2, 512, 128], P('mode', None, 'space')
- solution_new: float32 [32, 2, 512, 128], P('mode', None, 'space')
- residual_new: float32 [32, 2, 512, 128], P('mode', None, 'space')
- direction_new: float32 [32, 2, 512, 128], P('mode', None, 'space')
The draws below stay inside these ranges and needn't reach their ends.
Inputs may be any that keep to these rules, and one draw needn't show every extreme that they name: kl_terms[0] is positive everywhere.
All inputs are finite; a program needn't handle non-finite values.
Results may differ from the reference program's by a relative error of at most 0.00018.
Values sent between devices are 32-bit elements; how exact they have to be, the bound alone decides.
A program may use at most 64 MiB of HBM per device.

```python
import jax
import jax.numpy as jnp
from jax import lax

KL = 21
TERMS = 24
NY = 128
NZ = 2
MODES = 32
NX = 512


def draw_kl_terms(key, part):
    key = jax.random.fold_in(key, 11)
    mean_key, vary_key = jax.random.split(key, 2)
    extent = (KL, NZ, NX, NY)
    term_order = jnp.arange(KL).reshape(KL, 1, 1, 1)
    mean_field = jax.random.uniform(mean_key, extent, jnp.float32, 1.0, 2.0)
    varied = jnp.clip(0.5 * jax.random.normal(vary_key, extent, jnp.float32), -2.5, 2.5)
    return jnp.where(term_order == 0, mean_field, varied)


def with_ends(array, rng, least, high):
    spot = [jax.random.randint(jax.random.fold_in(rng, axis), (), 0, length) for axis, length in enumerate(array.shape)]
    main_axis = array.shape.index(max(array.shape))
    beside = spot[:main_axis] + [(spot[main_axis] + 1) % array.shape[main_axis]] + spot[main_axis + 1:]
    return array.at[tuple(spot)].set(least).at[tuple(beside)].set(high)


def shard_levels(key, shape, cuts, low, high):
    def one(dim, shards_of):
        heights = jax.random.uniform(jax.random.fold_in(jax.random.fold_in(key, 6), dim), (shards_of,), jnp.float32, low / len(cuts), high / len(cuts))
        return jnp.repeat(jnp.exp(heights), shape[dim] // shards_of).reshape((-1,) + (1,) * (len(shape) - dim - 1))

    gain = one(*cuts[0])
    for cut in cuts[1:]:
        gain = gain * one(*cut)
    return gain


def normal_values(own_key, shape, width, most, pieces=(), held_as=jnp.bfloat16):
    drawn = jax.random.normal(own_key, shape, jnp.float32) * width
    if len(pieces) > 0:
        drawn = shard_levels(own_key, shape, pieces, -0.22, 0.18) * drawn
    return jnp.clip(drawn, min=-most, max=most).astype(held_as)


def setup_inputs(seed: int = 0) -> dict:
    seeds = jax.random.split(jax.random.key(seed), 7)
    return {
        "residual": normal_values(seeds[0], (MODES, NZ, NX, NY), 1.0, 6.0, ((0, 16), (2, 32)), jnp.float32),
        "solution": normal_values(seeds[1], (MODES, NZ, NX, NY), 1.0, 6.0, ((0, 16), (2, 32)), jnp.float32),
        "kl_terms": draw_kl_terms(jax.random.fold_in(seeds[6], 71), 0),
        "partner": with_ends(jax.random.randint(seeds[3], (MODES, TERMS), 0, MODES), jax.random.fold_in(seeds[3], 1), 0, MODES - 1).astype(jnp.int32),
        "kl_index": with_ends(jax.random.randint(seeds[4], (MODES, TERMS), 1, KL), jax.random.fold_in(seeds[4], 1), 1, KL - 1).astype(jnp.int32),
        "coefficient": normal_values(seeds[5], (MODES, TERMS), 0.3, 4.0, ((0, 16),), jnp.float32),
    }


EPS = 1e-6


def diffuse(values, coeffs):
    pad_v = [(0, 0)] * (values.ndim - 3) + [(1, 1), (0, 0), (1, 1)]
    pad_c = [(0, 0)] * (coeffs.ndim - 3) + [(1, 1), (0, 0), (1, 1)]
    full_v = jnp.pad(values, pad_v)
    full_c = jnp.pad(coeffs, pad_c)
    centre_val = full_v[..., 1:-1, 1:-1, 1:-1]
    centre_cof = full_c[..., 1:-1, 1:-1, 1:-1]
    beside_val = [full_v[..., 2:, 1:-1, 1:-1], full_v[..., :-2, 1:-1, 1:-1], full_v[..., 1:-1, 2:, 1:-1], full_v[..., 1:-1, :-2, 1:-1], full_v[..., 1:-1, 1:-1, 2:], full_v[..., 1:-1, 1:-1, :-2]]
    beside_cof = [full_c[..., 2:, 1:-1, 1:-1], full_c[..., :-2, 1:-1, 1:-1], full_c[..., 1:-1, 2:, 1:-1], full_c[..., 1:-1, :-2, 1:-1], full_c[..., 1:-1, 1:-1, 2:], full_c[..., 1:-1, 1:-1, :-2]]
    total = 0.5 * (centre_cof + beside_cof[0]) * (centre_val - beside_val[0])
    for near_v, near_c in zip(beside_val[1:], beside_cof[1:]):
        total = total + 0.5 * (centre_cof + near_c) * (centre_val - near_v)
    return total


def reference(residual, solution, kl_terms, partner, kl_index, coefficient):
    padded = jnp.pad(residual, ((0, 0), (0, 0), (1, 1), (0, 0)))
    coef_pad = jnp.pad(kl_terms, ((0, 0), (0, 0), (1, 1), (0, 0)))
    image_self = diffuse(padded, coef_pad[0])

    def one_row(entries):
        part_row, term_row, weight_row = entries
        fields = padded[part_row]
        local_cof = coef_pad[term_row]
        return jnp.sum(weight_row[:, None, None, None] * diffuse(fields, local_cof), axis=0)

    couple = lax.map(one_row, (partner, kl_index, coefficient))
    image = image_self + couple
    norm_old = jnp.sum(residual * residual)
    curve = jnp.sum(residual * image)
    energy = jnp.sum(image * image)
    step_size = curve / (energy + EPS)
    solution_new = solution + step_size * residual
    residual_new = residual - step_size * image
    norm_new = jnp.sum(residual_new * residual_new)
    direction_new = residual_new + (norm_new / (norm_old + EPS)) * residual
    return (image, solution_new, residual_new, direction_new)
```

```python
import jax
import jax.numpy as jnp
from jax import lax
from jax.experimental import pallas as pl
from jax.experimental.pallas import tpu as pltpu
from jax.sharding import PartitionSpec as P

EPS = 1e-6
MESH = pl.DeviceIdType.MESH
KL, TERMS, MODES = 21, 24, 32
F32 = jnp.float32


def group_shift(t, sign=1):
    m, s = lax.axis_index("mode"), lax.axis_index("space")
    xh = (m // 8 + 1 - t // 8) % 2
    y = (m // 2 + sign * ((t // 2 + 1) % 4) + 4) % 4
    c = (m + 1 - t % 2) % 2
    return xh * 8 + y * 2 + c, s


def half_shift(t, sign=1):
    m, s = lax.axis_index("mode"), lax.axis_index("space")
    y = (m // 2 + sign * ((t // 2 + 1) % 4) + 4) % 4
    c = (m + 1 - t % 2) % 2
    return (m // 8) * 8 + y * 2 + c, s


def plane_shift(t):
    m, s = lax.axis_index("mode"), lax.axis_index("space")
    x = ((m // 8) * 2 + s // 16 + t // 8 + 1) % 4
    y = (m // 2 + t // 2 + 1) % 4
    c = (m + 1 - t % 2) % 2
    return (x // 2) * 8 + y * 2 + c, (x % 2) * 16 + s % 16


def z_shift(t):
    m, s = lax.axis_index("mode"), lax.axis_index("space")
    return m, (s // 16) * 16 + (s + jnp.where(t < 8, 8 - t, t + 1)) % 16


def loop(n, body):
    def step(t, carry):
        body(t)
        return carry

    lax.fori_loop(0, n, step, 0)


def galerkin(
    res_hbm, kl_hbm, part_hbm, term_hbm, coef_hbm,
    image_ref, sums_ref,
    res, klv, part_v, term_v, coef_v,
    pieces, edges, kl_edge, ints, floats,
    got, got_edges, got_kl, got_ints, got_floats, int_s, float_s,
    cof, aa, ff, img, back, sum_a, sums_a, sum_b, sums_b,
    in_sem, main_ss, main_rs, edge_ss, edge_rs, kle_ss, kle_rs,
    int_ss, int_rs, flo_ss, flo_rs, smem_sem,
    a_ss, a_rs, b_ss, b_rs, back_ss, back_rs,
):
    m, s = lax.axis_index("mode"), lax.axis_index("space")
    g, q = m // 8, m % 8
    own_plane = ((m // 8) * 2 + s // 16) * 8 + m % 8
    z_at = s % 16
    low, high = s > 0, s < 31
    first, last = q == 0, q == 7
    get_low, get_high = first & low, last & high
    get_edge = get_low | get_high
    put_kl = (first & high) | (last & low)

    loads = [
        pltpu.make_async_copy(a, b, in_sem.at[i])
        for i, (a, b) in enumerate(
            (
                (res_hbm, res.at[:, :, 8:24, :]),
                (part_hbm, part_v),
                (term_hbm, term_v),
                (coef_hbm, coef_v),
                (kl_hbm, klv.at[:, :, 8:24, :]),
            )
        )
    ]
    for load in loads:
        load.start()

    barrier = pltpu.get_barrier_semaphore()

    def greet(device):
        pl.semaphore_signal(barrier, inc=1, device_id=device, device_id_type=MESH)

    loop(15, lambda t: greet(z_shift(t)))
    loop(31, lambda t: greet(plane_shift(t)))

    @pl.when(get_low)
    def _():
        loop(16, lambda t: greet((t, jnp.maximum(s - 1, 0))))

    @pl.when(get_high)
    def _():
        loop(16, lambda t: greet((t, jnp.minimum(s + 1, 31))))

    for load in loads[:4]:
        load.wait()
    for i in range(2):
        for z in range(2):
            res[i, z, 0:8, :] = jnp.zeros((8, 128), F32)
            res[i, z, 24:32, :] = jnp.zeros((8, 128), F32)
    for j in range(8):
        for i in range(2):
            for z in range(2):
                pieces[j, i, 4 * z : 4 * z + 4, :] = res[i, z, 2 * j + 7 : 2 * j + 11, :]
    for i in range(2):
        for z in range(2):
            edges[0, 2 * i + z : 2 * i + z + 1, :] = res[i, z, 23:24, :]
            edges[1, 2 * i + z : 2 * i + z + 1, :] = res[i, z, 8:9, :]
    ints[0, :, 0:TERMS] = part_v[...]
    ints[1, :, 0:TERMS] = term_v[...]
    floats[:, 0:TERMS] = coef_v[...]
    loads[4].wait()
    end = jnp.where(first, 23, 8)
    for z in range(2):
        kl_edge[:, z : z + 1, :] = klv[:, z, pl.ds(end, 1), :]

    pl.semaphore_wait(barrier, 46 + 2 * low.astype(jnp.int32) + 2 * high.astype(jnp.int32))

    def main_copy(t):
        to = group_shift(t)
        return pltpu.make_async_remote_copy(
            src_ref=pieces.at[to[0] % 8], dst_ref=got.at[m], send_sem=main_ss.at[t], recv_sem=main_rs.at[t],
            device_id=to, device_id_type=MESH,
        )

    def edge_copy(up, half):
        to = (half * 8, jnp.minimum(s + 1, 31)) if up else (half * 8 + 7, jnp.maximum(s - 1, 0))
        return pltpu.make_async_remote_copy(
            src_ref=edges.at[0 if up else 1], dst_ref=got_edges.at[m], send_sem=edge_ss.at[(0 if up else 2) + half],
            recv_sem=edge_rs.at[m], device_id=to, device_id_type=MESH,
        )

    def kl_copy():
        return pltpu.make_async_remote_copy(
            src_ref=kl_edge, dst_ref=got_kl, send_sem=kle_ss, recv_sem=kle_rs,
            device_id=(m, jnp.where(first, jnp.minimum(s + 1, 31), jnp.maximum(s - 1, 0))), device_id_type=MESH,
        )

    def int_copy(t):
        return pltpu.make_async_remote_copy(
            src_ref=ints, dst_ref=got_ints.at[q], send_sem=int_ss.at[t], recv_sem=int_rs.at[t],
            device_id=half_shift(t), device_id_type=MESH,
        )

    def float_copy(t):
        return pltpu.make_async_remote_copy(
            src_ref=floats, dst_ref=got_floats.at[q], send_sem=flo_ss.at[t], recv_sem=flo_rs.at[t],
            device_id=half_shift(t), device_id_type=MESH,
        )

    @pl.when(put_kl)
    def _():
        kl_copy().start()

    @pl.when(high)
    def _():
        edge_copy(True, 0).start()
        edge_copy(True, 1).start()

    @pl.when(low)
    def _():
        edge_copy(False, 0).start()
        edge_copy(False, 1).start()

    loop(15, lambda t: main_copy(t).start())

    def start_tables(t):
        int_copy(t).start()
        float_copy(t).start()

    loop(7, start_tables)

    got[m] = pieces[q]
    got_ints[q] = ints[...]
    got_floats[q] = floats[...]

    for z in range(2):
        for r in range(4):
            cof[:, 4 * z + r : 4 * z + r + 1, :] = klv[:, z, pl.ds(2 * q + 7 + r, 1), :]

    @pl.when(first)
    def _():
        cof[:, 0:1, :] = jnp.zeros((KL, 1, 128), F32)
        cof[:, 4:5, :] = jnp.zeros((KL, 1, 128), F32)

    @pl.when(last)
    def _():
        cof[:, 3:4, :] = jnp.zeros((KL, 1, 128), F32)
        cof[:, 7:8, :] = jnp.zeros((KL, 1, 128), F32)

    @pl.when(get_edge)
    def _():
        kl_copy().wait_recv()

    @pl.when(get_low)
    def _():
        cof[:, 0:1, :] = got_kl[:, 0:1, :]
        cof[:, 4:5, :] = got_kl[:, 1:2, :]

    @pl.when(get_high)
    def _():
        cof[:, 3:4, :] = got_kl[:, 0:1, :]
        cof[:, 7:8, :] = got_kl[:, 1:2, :]

    lane = lax.broadcasted_iota(jnp.int32, (8, 128), 1)
    sub = lax.broadcasted_iota(jnp.int32, (8, 128), 0)
    inner = jnp.where(lane < 127, 0.5, 0.0).astype(F32)
    border = (0.5 + jnp.where(lane == 0, 0.5, 0.0) + jnp.where(lane == 127, 0.5, 0.0)).astype(F32)
    valid = (sub % 4 == 1) | (sub % 4 == 2)

    def coefficients(k):
        a = cof[k]
        aa[k, 0] = 0.5 * (a + pltpu.roll(a, 7, 0))
        aa[k, 1] = inner * (a + pltpu.roll(a, 127, 1))
        aa[k, 2] = 0.5 * (a + pltpu.roll(a, 4, 0))
        aa[k, 3] = border * a

    loop(KL, coefficients)

    def take_tables(t):
        int_copy(t).wait_recv()
        float_copy(t).wait_recv()

    loop(7, take_tables)
    to_smem = [
        pltpu.make_async_copy(got_ints, int_s, smem_sem.at[0]),
        pltpu.make_async_copy(got_floats, float_s, smem_sem.at[1]),
    ]
    for copy in to_smem:
        copy.start()

    loop(15, lambda t: main_copy(t).wait_recv())

    @pl.when(get_edge)
    def _():
        def take_edge(t):
            pltpu.make_async_remote_copy(
                src_ref=edges.at[0], dst_ref=got_edges.at[t], send_sem=edge_ss.at[0], recv_sem=edge_rs.at[t],
                device_id=(m, s), device_id_type=MESH,
            ).wait_recv()

        loop(16, take_edge)

    @pl.when(get_low)
    def _():
        for i in range(2):
            for z in range(2):
                got[:, i, 4 * z : 4 * z + 1, :] = got_edges[:, 2 * i + z : 2 * i + z + 1, :]

    @pl.when(get_high)
    def _():
        for i in range(2):
            for z in range(2):
                got[:, i, 4 * z + 3 : 4 * z + 4, :] = got_edges[:, 2 * i + z : 2 * i + z + 1, :]

    def differences(d):
        for i in range(2):
            v = got[d, i]
            ff[2 * d + i, 0] = v - pltpu.roll(v, 7, 0)
            ff[2 * d + i, 1] = v - pltpu.roll(v, 127, 1)
            ff[2 * d + i, 2] = v - pltpu.roll(v, 4, 0)
            ff[2 * d + i, 3] = v

    loop(16, differences)
    for copy in to_smem:
        copy.wait()

    def one_mode(n, carry):
        norm, curve, energy = carry
        own = g * 16 + n
        flux_x = aa[0, 0] * ff[own, 0]
        flux_y = aa[0, 1] * ff[own, 1]
        rest = aa[0, 2] * ff[own, 2] + aa[0, 3] * ff[own, 3]
        for e in range(TERMS):
            p = int_s[n // 2, 0, n % 2, e] & 31
            k = int_s[n // 2, 1, n % 2, e] & 31
            w = float_s[n // 2, n % 2, e]
            flux_x += w * (aa[k, 0] * ff[p, 0])
            flux_y += w * (aa[k, 1] * ff[p, 1])
            rest += w * (aa[k, 2] * ff[p, 2] + aa[k, 3] * ff[p, 3])
        out = rest + (flux_x - pltpu.roll(flux_x, 1, 0)) + (flux_y - pltpu.roll(flux_y, 1, 1))
        img[n] = out
        out = jnp.where(valid, out, 0.0)
        v = jnp.where(valid, ff[own, 3], 0.0)
        return norm + v * v, curve + v * out, energy + out * out

    zero = jnp.zeros((8, 128), F32)
    parts = lax.fori_loop(0, 16, one_mode, (zero, zero, zero))

    sum_a[...] = jnp.zeros((4, 128), F32)
    for i in range(3):
        sum_a[i : i + 1, :] = jnp.sum(parts[i], axis=0, keepdims=True)

    def a_copy(t):
        return pltpu.make_async_remote_copy(
            src_ref=sum_a, dst_ref=sums_a.at[own_plane], send_sem=a_ss.at[t], recv_sem=a_rs.at[t],
            device_id=plane_shift(t), device_id_type=MESH,
        )

    def b_copy(t):
        return pltpu.make_async_remote_copy(
            src_ref=sum_b, dst_ref=sums_b.at[z_at], send_sem=b_ss.at[t], recv_sem=b_rs.at[t],
            device_id=z_shift(t), device_id_type=MESH,
        )

    def back_copy(t):
        to = half_shift(t)
        return pltpu.make_async_remote_copy(
            src_ref=img.at[pl.ds(2 * (to[0] % 8), 2)], dst_ref=back.at[q], send_sem=back_ss.at[t], recv_sem=back_rs.at[t],
            device_id=to, device_id_type=MESH,
        )

    loop(31, lambda t: a_copy(t).start())
    sums_a[own_plane] = sum_a[...]
    loop(31, lambda t: a_copy(t).wait_recv())
    sum_b[...] = jnp.sum(sums_a[...], axis=0)
    loop(15, lambda t: b_copy(t).start())
    loop(7, lambda t: back_copy(t).start())
    sums_b[z_at] = sum_b[...]
    back[q] = img[pl.ds(2 * q, 2)]

    loop(7, lambda t: back_copy(t).wait_recv())
    for i in range(2):
        for z in range(2):
            for h in range(2):
                tile = pltpu.roll(back[4 * h, i], 7 - 4 * z, 0)
                for j in range(1, 4):
                    tile = jnp.where(sub // 2 == j, pltpu.roll(back[4 * h + j, i], (2 * j + 7 - 4 * z) % 8, 0), tile)
                image_ref[i, z, 8 * h : 8 * h + 8, :] = tile

    loop(15, lambda t: main_copy(t).wait_send())

    def tables_left(t):
        int_copy(t).wait_send()
        float_copy(t).wait_send()
        back_copy(t).wait_send()

    loop(7, tables_left)
    loop(31, lambda t: a_copy(t).wait_send())

    @pl.when(put_kl)
    def _():
        kl_copy().wait_send()

    @pl.when(high)
    def _():
        edge_copy(True, 0).wait_send()
        edge_copy(True, 1).wait_send()

    @pl.when(low)
    def _():
        edge_copy(False, 0).wait_send()
        edge_copy(False, 1).wait_send()

    loop(15, lambda t: b_copy(t).wait_recv())
    sums_ref[...] = jnp.sum(sums_b[...], axis=0)
    loop(15, lambda t: b_copy(t).wait_send())


def update(image_in, sums_ref, res_ref, sol_ref, image_ref, sol_out, res_out, dir_out):
    sums = jnp.sum(sums_ref[...], axis=1, keepdims=True)
    norm, curve, energy = sums[0:1], sums[1:2], sums[2:3]
    step = curve / (energy + EPS)
    norm_new = jnp.maximum(norm - 2.0 * step * curve + step * step * energy, 0.0)
    beta = norm_new / (norm + EPS)
    image = image_in[...].reshape(64, 128)
    r = res_ref[...].reshape(64, 128)
    image_ref[...] = image_in[...]
    sol_out[...] = (sol_ref[...].reshape(64, 128) + step * r).reshape(2, 2, 16, 128)
    r_new = r - step * image
    res_out[...] = r_new.reshape(2, 2, 16, 128)
    dir_out[...] = (r_new + beta * r).reshape(2, 2, 16, 128)


def on_device(residual, solution, kl_terms, partner, kl_index, coefficient):
    vmem = pl.BlockSpec(memory_space=pltpu.VMEM)
    anywhere = pl.BlockSpec(memory_space=pl.ANY)
    dma = pltpu.SemaphoreType.DMA
    field = jax.ShapeDtypeStruct(residual.shape, F32)
    i32 = jnp.int32
    image, sums = pl.pallas_call(
        galerkin,
        out_shape=(field, jax.ShapeDtypeStruct((4, 128), F32)),
        in_specs=[anywhere] * 5,
        out_specs=(vmem, vmem),
        scratch_shapes=[
            pltpu.VMEM((2, 2, 32, 128), F32),
            pltpu.VMEM((KL, 2, 32, 128), F32),
            pltpu.VMEM((2, TERMS), i32),
            pltpu.VMEM((2, TERMS), i32),
            pltpu.VMEM((2, TERMS), F32),
            pltpu.VMEM((8, 2, 8, 128), F32),
            pltpu.VMEM((2, 4, 128), F32),
            pltpu.VMEM((KL, 2, 128), F32),
            pltpu.VMEM((2, 2, 128), i32),
            pltpu.VMEM((2, 128), F32),
            pltpu.VMEM((16, 2, 8, 128), F32),
            pltpu.VMEM((16, 4, 128), F32),
            pltpu.VMEM((KL, 2, 128), F32),
            pltpu.VMEM((8, 2, 2, 128), i32),
            pltpu.VMEM((8, 2, 128), F32),
            pltpu.SMEM((8, 2, 2, 128), i32),
            pltpu.SMEM((8, 2, 128), F32),
            pltpu.VMEM((KL, 8, 128), F32),
            pltpu.VMEM((32, 4, 8, 128), F32),
            pltpu.VMEM((MODES, 4, 8, 128), F32),
            pltpu.VMEM((16, 8, 128), F32),
            pltpu.VMEM((8, 2, 8, 128), F32),
            pltpu.VMEM((4, 128), F32),
            pltpu.VMEM((32, 4, 128), F32),
            pltpu.VMEM((4, 128), F32),
            pltpu.VMEM((16, 4, 128), F32),
            dma((5,)),
            dma((15,)), dma((15,)),
            dma((4,)), dma((16,)),
            dma, dma,
            dma((7,)), dma((7,)),
            dma((7,)), dma((7,)),
            dma((2,)),
            dma((31,)), dma((31,)),
            dma((15,)), dma((15,)),
            dma((7,)), dma((7,)),
        ],
        compiler_params=pltpu.CompilerParams(
            collective_id=0, has_side_effects=True, vmem_limit_bytes=60 << 20
        ),
        name="galerkin",
    )(residual, kl_terms, partner, kl_index, coefficient)
    return pl.pallas_call(
        update,
        out_shape=(field, field, field, field),
        in_specs=[vmem] * 4,
        out_specs=(vmem,) * 4,
        compiler_params=pltpu.CompilerParams(vmem_limit_bytes=60 << 20),
        name="update",
    )(image, sums, residual, solution)


def solution(mesh):
    field = P("mode", None, "space", None)
    row = P("mode", None)
    return jax.shard_map(
        on_device,
        mesh=mesh,
        in_specs=(field, field, P(None, None, "space", None), row, row, row),
        out_specs=(field, field, field, field),
        check_vma=False,
    )
```

```python
import jax
import jax.numpy as jnp
from jax import lax
from jax.experimental import pallas as pl
from jax.experimental.pallas import tpu as pltpu
from jax.sharding import PartitionSpec as P

EPS = 1e-6
MESH = pl.DeviceIdType.MESH
KL, TERMS, MODES = 21, 24, 32
F32 = jnp.float32


def group_shift(t, sign=1):
    m, s = lax.axis_index("mode"), lax.axis_index("space")
    xh = (m // 8 + 1 - t // 8) % 2
    y = (m // 2 + sign * ((t // 2 + 1) % 4) + 4) % 4
    c = (m + 1 - t % 2) % 2
    return xh * 8 + y * 2 + c, s


def half_shift(t, sign=1):
    m, s = lax.axis_index("mode"), lax.axis_index("space")
    y = (m // 2 + sign * ((t // 2 + 1) % 4) + 4) % 4
    c = (m + 1 - t % 2) % 2
    return (m // 8) * 8 + y * 2 + c, s


def plane_shift(t):
    m, s = lax.axis_index("mode"), lax.axis_index("space")
    x = ((m // 8) * 2 + s // 16 + t // 8 + 1) % 4
    y = (m // 2 + t // 2 + 1) % 4
    c = (m + 1 - t % 2) % 2
    return (x // 2) * 8 + y * 2 + c, (x % 2) * 16 + s % 16


def z_shift(t):
    m, s = lax.axis_index("mode"), lax.axis_index("space")
    return m, (s // 16) * 16 + (s + jnp.where(t < 8, 8 - t, t + 1)) % 16


def along_z(d):
    m, s = lax.axis_index("mode"), lax.axis_index("space")
    return m, (s // 16) * 16 + (s + d + 16) % 16


def loop(n, body):
    def step(t, carry):
        body(t)
        return carry

    lax.fori_loop(0, n, step, 0)


def galerkin(
    res_hbm, sol_hbm, kl_hbm, part_hbm, term_hbm, coef_hbm,
    image_ref, sol_ref, res_ref, dir_ref,
    res, sol, klv, part_v, term_v, coef_v,
    pieces, edges, kl_edge, ints, floats,
    got, got_edges, got_kl, got_ints, got_floats, int_s, float_s,
    cof, aa, ff, img, back, sum_a, sums_a, sum_b, sums_b,
    in_sem, main_ss, main_rs, edge_ss, edge_rs, kle_ss, kle_rs,
    int_ss, int_rs, flo_ss, flo_rs, smem_sem,
    a_ss, a_rs, b_ss, b_rs, back_ss, back_rs, ring_sem,
):
    m, s = lax.axis_index("mode"), lax.axis_index("space")
    g, q = m // 8, m % 8
    own_plane = ((m // 8) * 2 + s // 16) * 8 + m % 8
    z_at = s % 16
    low, high = s > 0, s < 31
    first, last = q == 0, q == 7
    get_low, get_high = first & low, last & high
    get_edge = get_low | get_high
    put_kl = (first & high) | (last & low)

    loads = [
        pltpu.make_async_copy(a, b, in_sem.at[i])
        for i, (a, b) in enumerate(
            (
                (res_hbm, res.at[:, :, 8:24, :]),
                (part_hbm, part_v),
                (term_hbm, term_v),
                (coef_hbm, coef_v),
                (kl_hbm, klv.at[:, :, 8:24, :]),
                (sol_hbm, sol),
            )
        )
    ]
    for load in loads:
        load.start()

    barrier = pltpu.get_barrier_semaphore()

    def greet(device):
        pl.semaphore_signal(barrier, inc=1, device_id=device, device_id_type=MESH)

    greet(along_z(1))
    greet(along_z(-1))
    loop(31, lambda t: greet(plane_shift(t)))

    @pl.when(get_low)
    def _():
        loop(16, lambda t: greet((t, jnp.maximum(s - 1, 0))))

    @pl.when(get_high)
    def _():
        loop(16, lambda t: greet((t, jnp.minimum(s + 1, 31))))

    for load in loads[:4]:
        load.wait()
    for i in range(2):
        for z in range(2):
            res[i, z, 0:8, :] = jnp.zeros((8, 128), F32)
            res[i, z, 24:32, :] = jnp.zeros((8, 128), F32)
    for j in range(8):
        for i in range(2):
            for z in range(2):
                pieces[j, i, 4 * z : 4 * z + 4, :] = res[i, z, 2 * j + 7 : 2 * j + 11, :]
    for i in range(2):
        for z in range(2):
            edges[0, 2 * i + z : 2 * i + z + 1, :] = res[i, z, 23:24, :]
            edges[1, 2 * i + z : 2 * i + z + 1, :] = res[i, z, 8:9, :]
    ints[0, :, 0:TERMS] = part_v[...]
    ints[1, :, 0:TERMS] = term_v[...]
    floats[:, 0:TERMS] = coef_v[...]
    loads[4].wait()
    end = jnp.where(first, 23, 8)
    for z in range(2):
        kl_edge[:, z : z + 1, :] = klv[:, z, pl.ds(end, 1), :]

    pl.semaphore_wait(barrier, 33 + 2 * low.astype(jnp.int32) + 2 * high.astype(jnp.int32))

    def tell(i):
        for d in (1 << i, -(1 << i)):
            pl.semaphore_signal(ring_sem.at[i], inc=1, device_id=along_z(d), device_id_type=MESH)

    def hear(i):
        pl.semaphore_wait(ring_sem.at[i], 2)

    tell(0)

    def main_copy(t):
        to = group_shift(t)
        return pltpu.make_async_remote_copy(
            src_ref=pieces.at[to[0] % 8], dst_ref=got.at[m], send_sem=main_ss.at[t], recv_sem=main_rs.at[t],
            device_id=to, device_id_type=MESH,
        )

    def edge_copy(up, half):
        to = (half * 8, jnp.minimum(s + 1, 31)) if up else (half * 8 + 7, jnp.maximum(s - 1, 0))
        return pltpu.make_async_remote_copy(
            src_ref=edges.at[0 if up else 1], dst_ref=got_edges.at[m], send_sem=edge_ss.at[(0 if up else 2) + half],
            recv_sem=edge_rs.at[m], device_id=to, device_id_type=MESH,
        )

    def kl_copy():
        return pltpu.make_async_remote_copy(
            src_ref=kl_edge, dst_ref=got_kl, send_sem=kle_ss, recv_sem=kle_rs,
            device_id=(m, jnp.where(first, jnp.minimum(s + 1, 31), jnp.maximum(s - 1, 0))), device_id_type=MESH,
        )

    def int_copy(t):
        return pltpu.make_async_remote_copy(
            src_ref=ints, dst_ref=got_ints.at[q], send_sem=int_ss.at[t], recv_sem=int_rs.at[t],
            device_id=half_shift(t), device_id_type=MESH,
        )

    def float_copy(t):
        return pltpu.make_async_remote_copy(
            src_ref=floats, dst_ref=got_floats.at[q], send_sem=flo_ss.at[t], recv_sem=flo_rs.at[t],
            device_id=half_shift(t), device_id_type=MESH,
        )

    @pl.when(put_kl)
    def _():
        kl_copy().start()

    @pl.when(high)
    def _():
        edge_copy(True, 0).start()
        edge_copy(True, 1).start()

    @pl.when(low)
    def _():
        edge_copy(False, 0).start()
        edge_copy(False, 1).start()

    loop(15, lambda t: main_copy(t).start())

    def start_tables(t):
        int_copy(t).start()
        float_copy(t).start()

    loop(7, start_tables)

    hear(0)
    tell(1)
    got[m] = pieces[q]
    got_ints[q] = ints[...]
    got_floats[q] = floats[...]

    for z in range(2):
        for r in range(4):
            cof[:, 4 * z + r : 4 * z + r + 1, :] = klv[:, z, pl.ds(2 * q + 7 + r, 1), :]

    @pl.when(first)
    def _():
        cof[:, 0:1, :] = jnp.zeros((KL, 1, 128), F32)
        cof[:, 4:5, :] = jnp.zeros((KL, 1, 128), F32)

    @pl.when(last)
    def _():
        cof[:, 3:4, :] = jnp.zeros((KL, 1, 128), F32)
        cof[:, 7:8, :] = jnp.zeros((KL, 1, 128), F32)

    @pl.when(get_edge)
    def _():
        kl_copy().wait_recv()

    @pl.when(get_low)
    def _():
        cof[:, 0:1, :] = got_kl[:, 0:1, :]
        cof[:, 4:5, :] = got_kl[:, 1:2, :]

    @pl.when(get_high)
    def _():
        cof[:, 3:4, :] = got_kl[:, 0:1, :]
        cof[:, 7:8, :] = got_kl[:, 1:2, :]

    lane = lax.broadcasted_iota(jnp.int32, (8, 128), 1)
    sub = lax.broadcasted_iota(jnp.int32, (8, 128), 0)
    inner = jnp.where(lane < 127, 0.5, 0.0).astype(F32)
    border = (0.5 + jnp.where(lane == 0, 0.5, 0.0) + jnp.where(lane == 127, 0.5, 0.0)).astype(F32)
    valid = (sub % 4 == 1) | (sub % 4 == 2)

    def coefficients(k):
        a = cof[k]
        aa[k, 0] = 0.5 * (a + pltpu.roll(a, 7, 0))
        aa[k, 1] = inner * (a + pltpu.roll(a, 127, 1))
        aa[k, 2] = 0.5 * (a + pltpu.roll(a, 4, 0))
        aa[k, 3] = border * a

    loop(KL, coefficients)

    hear(1)
    tell(2)

    def take_tables(t):
        int_copy(t).wait_recv()
        float_copy(t).wait_recv()

    loop(7, take_tables)
    to_smem = [
        pltpu.make_async_copy(got_ints, int_s, smem_sem.at[0]),
        pltpu.make_async_copy(got_floats, float_s, smem_sem.at[1]),
    ]
    for copy in to_smem:
        copy.start()

    loop(15, lambda t: main_copy(t).wait_recv())

    @pl.when(get_edge)
    def _():
        def take_edge(t):
            pltpu.make_async_remote_copy(
                src_ref=edges.at[0], dst_ref=got_edges.at[t], send_sem=edge_ss.at[0], recv_sem=edge_rs.at[t],
                device_id=(m, s), device_id_type=MESH,
            ).wait_recv()

        loop(16, take_edge)

    @pl.when(get_low)
    def _():
        for i in range(2):
            for z in range(2):
                got[:, i, 4 * z : 4 * z + 1, :] = got_edges[:, 2 * i + z : 2 * i + z + 1, :]

    @pl.when(get_high)
    def _():
        for i in range(2):
            for z in range(2):
                got[:, i, 4 * z + 3 : 4 * z + 4, :] = got_edges[:, 2 * i + z : 2 * i + z + 1, :]

    def differences(d):
        for i in range(2):
            v = got[d, i]
            ff[2 * d + i, 0] = v - pltpu.roll(v, 7, 0)
            ff[2 * d + i, 1] = v - pltpu.roll(v, 127, 1)
            ff[2 * d + i, 2] = v - pltpu.roll(v, 4, 0)
            ff[2 * d + i, 3] = v

    loop(16, differences)
    for copy in to_smem:
        copy.wait()

    def one_mode(n, carry):
        norm, curve, energy = carry
        own = g * 16 + n
        flux_x = aa[0, 0] * ff[own, 0]
        flux_y = aa[0, 1] * ff[own, 1]
        rest = aa[0, 2] * ff[own, 2] + aa[0, 3] * ff[own, 3]
        for e in range(TERMS):
            p = int_s[n // 2, 0, n % 2, e] & 31
            k = int_s[n // 2, 1, n % 2, e] & 31
            w = float_s[n // 2, n % 2, e]
            flux_x += w * (aa[k, 0] * ff[p, 0])
            flux_y += w * (aa[k, 1] * ff[p, 1])
            rest += w * (aa[k, 2] * ff[p, 2] + aa[k, 3] * ff[p, 3])
        out = rest + (flux_x - pltpu.roll(flux_x, 1, 0)) + (flux_y - pltpu.roll(flux_y, 1, 1))
        img[n] = out
        out = jnp.where(valid, out, 0.0)
        v = jnp.where(valid, ff[own, 3], 0.0)
        return norm + v * v, curve + v * out, energy + out * out

    zero = jnp.zeros((8, 128), F32)
    parts = lax.fori_loop(0, 16, one_mode, (zero, zero, zero))

    sum_a[...] = jnp.zeros((4, 128), F32)
    for i in range(3):
        sum_a[i : i + 1, :] = jnp.sum(parts[i], axis=0, keepdims=True)

    def a_copy(t):
        return pltpu.make_async_remote_copy(
            src_ref=sum_a, dst_ref=sums_a.at[own_plane], send_sem=a_ss.at[t], recv_sem=a_rs.at[t],
            device_id=plane_shift(t), device_id_type=MESH,
        )

    def b_copy(t):
        return pltpu.make_async_remote_copy(
            src_ref=sum_b, dst_ref=sums_b.at[z_at], send_sem=b_ss.at[t], recv_sem=b_rs.at[t],
            device_id=z_shift(t), device_id_type=MESH,
        )

    def back_copy(t):
        to = half_shift(t)
        return pltpu.make_async_remote_copy(
            src_ref=img.at[pl.ds(2 * (to[0] % 8), 2)], dst_ref=back.at[q], send_sem=back_ss.at[t], recv_sem=back_rs.at[t],
            device_id=to, device_id_type=MESH,
        )

    loop(31, lambda t: a_copy(t).start())
    sums_a[own_plane] = sum_a[...]
    loop(31, lambda t: a_copy(t).wait_recv())
    sum_b[...] = jnp.sum(sums_a[...], axis=0)
    hear(2)
    loop(15, lambda t: b_copy(t).start())
    loop(7, lambda t: back_copy(t).start())
    sums_b[z_at] = sum_b[...]
    back[q] = img[pl.ds(2 * q, 2)]

    loop(7, lambda t: back_copy(t).wait_recv())
    for i in range(2):
        for z in range(2):
            for h in range(2):
                tile = pltpu.roll(back[4 * h, i], 7 - 4 * z, 0)
                for j in range(1, 4):
                    tile = jnp.where(sub // 2 == j, pltpu.roll(back[4 * h + j, i], (2 * j + 7 - 4 * z) % 8, 0), tile)
                image_ref[i, z, 8 * h : 8 * h + 8, :] = tile

    loop(15, lambda t: main_copy(t).wait_send())

    def tables_left(t):
        int_copy(t).wait_send()
        float_copy(t).wait_send()
        back_copy(t).wait_send()

    loop(7, tables_left)
    loop(31, lambda t: a_copy(t).wait_send())

    @pl.when(put_kl)
    def _():
        kl_copy().wait_send()

    @pl.when(high)
    def _():
        edge_copy(True, 0).wait_send()
        edge_copy(True, 1).wait_send()

    @pl.when(low)
    def _():
        edge_copy(False, 0).wait_send()
        edge_copy(False, 1).wait_send()

    loads[5].wait()

    loop(15, lambda t: b_copy(t).wait_recv())
    sums = jnp.sum(jnp.sum(sums_b[...], axis=0), axis=1, keepdims=True)
    norm, curve, energy = sums[0:1], sums[1:2], sums[2:3]
    step = curve / (energy + EPS)
    norm_new = jnp.maximum(norm - 2.0 * step * curve + step * step * energy, 0.0)
    beta = norm_new / (norm + EPS)
    for i in range(2):
        for z in range(2):
            for h in range(2):
                rows = pl.ds(8 * h, 8)
                r = res[i, z, 8 + 8 * h : 16 + 8 * h, :]
                sol_ref[i, z, rows, :] = sol[i, z, rows, :] + step * r
                r_new = r - step * image_ref[i, z, rows, :]
                res_ref[i, z, rows, :] = r_new
                dir_ref[i, z, rows, :] = r_new + beta * r
    loop(15, lambda t: b_copy(t).wait_send())


def deliver(*refs):
    sem = refs[8]
    copies = [pltpu.make_async_copy(refs[i], refs[4 + i], sem.at[i]) for i in range(4)]
    for copy in copies:
        copy.start()
    for copy in copies:
        copy.wait()


def on_device(residual, solution, kl_terms, partner, kl_index, coefficient):
    vmem = pl.BlockSpec(memory_space=pltpu.VMEM)
    anywhere = pl.BlockSpec(memory_space=pl.ANY)
    dma = pltpu.SemaphoreType.DMA
    field = pltpu.VMEM(residual.shape, F32)
    i32 = jnp.int32
    results = pl.pallas_call(
        galerkin,
        out_shape=(field,) * 4,
        in_specs=[anywhere] * 6,
        out_specs=(vmem,) * 4,
        scratch_shapes=[
            pltpu.VMEM((2, 2, 32, 128), F32),
            pltpu.VMEM((2, 2, 16, 128), F32),
            pltpu.VMEM((KL, 2, 32, 128), F32),
            pltpu.VMEM((2, TERMS), i32),
            pltpu.VMEM((2, TERMS), i32),
            pltpu.VMEM((2, TERMS), F32),
            pltpu.VMEM((8, 2, 8, 128), F32),
            pltpu.VMEM((2, 4, 128), F32),
            pltpu.VMEM((KL, 2, 128), F32),
            pltpu.VMEM((2, 2, 128), i32),
            pltpu.VMEM((2, 128), F32),
            pltpu.VMEM((16, 2, 8, 128), F32),
            pltpu.VMEM((16, 4, 128), F32),
            pltpu.VMEM((KL, 2, 128), F32),
            pltpu.VMEM((8, 2, 2, 128), i32),
            pltpu.VMEM((8, 2, 128), F32),
            pltpu.SMEM((8, 2, 2, 128), i32),
            pltpu.SMEM((8, 2, 128), F32),
            pltpu.VMEM((KL, 8, 128), F32),
            pltpu.VMEM((32, 4, 8, 128), F32),
            pltpu.VMEM((MODES, 4, 8, 128), F32),
            pltpu.VMEM((16, 8, 128), F32),
            pltpu.VMEM((8, 2, 8, 128), F32),
            pltpu.VMEM((4, 128), F32),
            pltpu.VMEM((32, 4, 128), F32),
            pltpu.VMEM((4, 128), F32),
            pltpu.VMEM((16, 4, 128), F32),
            dma((6,)),
            dma((15,)), dma((15,)),
            dma((4,)), dma((16,)),
            dma, dma,
            dma((7,)), dma((7,)),
            dma((7,)), dma((7,)),
            dma((2,)),
            dma((31,)), dma((31,)),
            dma((15,)), dma((15,)),
            dma((7,)), dma((7,)),
            pltpu.SemaphoreType.REGULAR((3,)),
        ],
        compiler_params=pltpu.CompilerParams(
            collective_id=0, has_side_effects=True, vmem_limit_bytes=60 << 20
        ),
        name="galerkin",
    )(residual, solution, kl_terms, partner, kl_index, coefficient)
    return pl.pallas_call(
        deliver,
        out_shape=(jax.ShapeDtypeStruct(residual.shape, F32),) * 4,
        in_specs=[vmem] * 4,
        out_specs=(anywhere,) * 4,
        scratch_shapes=[dma((4,))],
        compiler_params=pltpu.CompilerParams(vmem_limit_bytes=60 << 20),
        name="deliver",
    )(*(pltpu.with_memory_space_constraint(a, pltpu.VMEM) for a in results))


def solution(mesh):
    field = P("mode", None, "space", None)
    row = P("mode", None)
    return jax.shard_map(
        on_device,
        mesh=mesh,
        in_specs=(field, field, P(None, None, "space", None), row, row, row),
        out_specs=(field, field, field, field),
        check_vma=False,
    )
```

```python
import jax
import jax.numpy as jnp
from jax import lax
from jax.experimental import pallas as pl
from jax.experimental.pallas import tpu as pltpu
from jax.sharding import PartitionSpec as P

EPS = 1e-6
MESH = pl.DeviceIdType.MESH
KL, TERMS, MODES = 21, 24, 32
F32 = jnp.float32


def hops(dx, dy):
    return min(dx, 4 - dx) + min(dy, 4 - dy)


GROUP = sorted(((a, b, d) for a in (0, 1) for b in range(4) for d in (0, 1) if a or b or d), key=lambda t: (-hops(2 * t[0], t[1]), -t[2]))
HALF = [t[1:] for t in GROUP if not t[0]]
PLANE = sorted(((a, b, d) for a in range(4) for b in range(4) for d in (0, 1) if a or b or d), key=lambda t: (-hops(t[0], t[1]), -t[2]))
RING = [8, 7, 9, 6, 10, 5, 11, 4, 12, 3, 13, 2, 14, 1, 15]


def galerkin(
    res_hbm, sol_hbm, kl_hbm, part_hbm, term_hbm, coef_hbm,
    image_ref, sol_ref, res_ref, dir_ref,
    res, sol, klv, part_v, term_v, coef_v,
    pieces, edges, kl_edge, ints, floats,
    got, got_edges, got_kl, got_ints, got_floats, int_s, float_s,
    cof, aa, wa, ff, img, back, sum_a, sums_a, sum_b, sums_b,
    in_sem, main_ss, main_rs, edge_ss, edge_rs, kle_ss, kle_rs,
    int_ss, int_rs, flo_ss, flo_rs, smem_sem,
    a_ss, a_rs, b_ss, b_rs, back_ss, back_rs, ring_sem,
):
    m, s = lax.axis_index("mode"), lax.axis_index("space")
    g, q = m // 8, m % 8
    xh, y, c, xl, z_at = g, (m // 2) % 4, m % 2, s // 16, s % 16
    ys = [(y + b) % 4 for b in range(4)]
    cs = [c, 1 - c]
    x_now = xh * 2 + xl
    xs = [(x_now + a) % 4 for a in range(4)]
    row_of = [[ys[b] * 2 + cs[d] for d in range(2)] for b in range(4)]
    half_of = [g * 8, (1 - g) * 8]
    chip_x = [((x // 2) * 8, (x % 2) * 16 + z_at) for x in xs]
    own_plane = x_now * 8 + q
    low, high = s > 0, s < 31
    first, last = q == 0, q == 7
    get_low, get_high = first & low, last & high
    get_edge = get_low | get_high
    put_kl = (first & high) | (last & low)
    below, above = jnp.maximum(s - 1, 0), jnp.minimum(s + 1, 31)

    loads = [
        pltpu.make_async_copy(a, b, in_sem.at[i])
        for i, (a, b) in enumerate(
            (
                (res_hbm, res.at[:, :, 8:24, :]),
                (part_hbm, part_v),
                (term_hbm, term_v),
                (coef_hbm, coef_v),
                (kl_hbm, klv.at[:, :, 8:24, :]),
                (sol_hbm, sol),
            )
        )
    ]
    for load in loads:
        load.start()

    barrier = pltpu.get_barrier_semaphore()

    def greet(device):
        pl.semaphore_signal(barrier, inc=1, device_id=device, device_id_type=MESH)

    def along_z(d):
        return m, xl * 16 + (z_at + d) % 16

    def in_plane(t):
        mode, space = chip_x[t[0]]
        return mode + row_of[t[1]][t[2]], space

    def in_half(t):
        return half_of[0] + row_of[t[0]][t[1]], s

    def in_group(t):
        return half_of[t[0]] + row_of[t[1]][t[2]], s

    def group_source(t):
        return half_of[t[0]] + row_of[(4 - t[1]) % 4][t[2]]

    @pl.when(get_low)
    def _():
        for t in range(16):
            greet((t, below))

    @pl.when(get_high)
    def _():
        for t in range(16):
            greet((t, above))

    for t in PLANE:
        greet(in_plane(t))
    greet(along_z(1))
    greet(along_z(15))

    for i in range(2):
        for z in range(2):
            res[i, z, 0:8, :] = jnp.zeros((8, 128), F32)
            res[i, z, 24:32, :] = jnp.zeros((8, 128), F32)
    loads[0].wait()
    for j in range(8):
        for i in range(2):
            for z in range(2):
                pieces[j, i, 4 * z : 4 * z + 4, :] = res[i, z, 2 * j + 7 : 2 * j + 11, :]
    for i in range(2):
        for z in range(2):
            edges[0, 2 * i + z : 2 * i + z + 1, :] = res[i, z, 23:24, :]
            edges[1, 2 * i + z : 2 * i + z + 1, :] = res[i, z, 8:9, :]
    for load in loads[1:4]:
        load.wait()
    ints[0, :, 0:TERMS] = (part_v[...] % 2) * 16 + part_v[...] // 2
    ints[1, :, 0:TERMS] = term_v[...]
    floats[:, 0:TERMS] = coef_v[...]

    pl.semaphore_wait(barrier, 33 + 2 * low.astype(jnp.int32) + 2 * high.astype(jnp.int32))

    def tell(i):
        for d in (1 << i, 16 - (1 << i)):
            pl.semaphore_signal(ring_sem.at[i], inc=1, device_id=along_z(d), device_id_type=MESH)

    def hear(i):
        pl.semaphore_wait(ring_sem.at[i], 2)

    def main_copy(i):
        to = in_group(GROUP[i])
        return pltpu.make_async_remote_copy(
            src_ref=pieces.at[row_of[GROUP[i][1]][GROUP[i][2]]], dst_ref=got.at[m], send_sem=main_ss, recv_sem=main_rs.at[i],
            device_id=to, device_id_type=MESH,
        )

    def edge_copy(up, half):
        to = (half * 8, above) if up else (half * 8 + 7, below)
        return pltpu.make_async_remote_copy(
            src_ref=edges.at[0 if up else 1], dst_ref=got_edges.at[m], send_sem=edge_ss.at[(0 if up else 2) + half],
            recv_sem=edge_rs, device_id=to, device_id_type=MESH,
        )

    def kl_copy():
        return pltpu.make_async_remote_copy(
            src_ref=kl_edge, dst_ref=got_kl, send_sem=kle_ss, recv_sem=kle_rs,
            device_id=(m, jnp.where(first, above, below)), device_id_type=MESH,
        )

    def int_copy(i):
        return pltpu.make_async_remote_copy(
            src_ref=ints, dst_ref=got_ints.at[q], send_sem=int_ss, recv_sem=int_rs,
            device_id=in_half(HALF[i]), device_id_type=MESH,
        )

    def float_copy(i):
        return pltpu.make_async_remote_copy(
            src_ref=floats, dst_ref=got_floats.at[q], send_sem=flo_ss, recv_sem=flo_rs,
            device_id=in_half(HALF[i]), device_id_type=MESH,
        )

    def all_of(ref, n, send_sem, recv_sem):
        return pltpu.make_async_remote_copy(
            src_ref=ref.at[pl.ds(0, n)], dst_ref=ref.at[pl.ds(0, n)], send_sem=send_sem, recv_sem=recv_sem,
            device_id=(m, s), device_id_type=MESH,
        )

    @pl.when(high)
    def _():
        edge_copy(True, 0).start()
        edge_copy(True, 1).start()

    @pl.when(low)
    def _():
        edge_copy(False, 0).start()
        edge_copy(False, 1).start()

    for i in range(15):
        main_copy(i).start()
    for i in range(7):
        int_copy(i).start()
        float_copy(i).start()
    tell(0)

    loads[4].wait()
    end = jnp.where(first, 23, 8)
    for z in range(2):
        kl_edge[:, z : z + 1, :] = klv[:, z, pl.ds(end, 1), :]

    @pl.when(put_kl)
    def _():
        kl_copy().start()

    hear(0)
    tell(1)

    for z in range(2):
        for r in range(4):
            cof[:, 4 * z + r : 4 * z + r + 1, :] = klv[:, z, pl.ds(2 * q + 7 + r, 1), :]

    @pl.when(first)
    def _():
        cof[:, 0:1, :] = jnp.zeros((KL, 1, 128), F32)
        cof[:, 4:5, :] = jnp.zeros((KL, 1, 128), F32)

    @pl.when(last)
    def _():
        cof[:, 3:4, :] = jnp.zeros((KL, 1, 128), F32)
        cof[:, 7:8, :] = jnp.zeros((KL, 1, 128), F32)

    lane = lax.broadcasted_iota(jnp.int32, (8, 128), 1)
    sub = lax.broadcasted_iota(jnp.int32, (8, 128), 0)
    inner = jnp.where(lane < 127, 0.5, 0.0).astype(F32)
    border = (0.5 + jnp.where(lane == 0, 0.5, 0.0) + jnp.where(lane == 127, 0.5, 0.0)).astype(F32)
    valid = (sub % 4 == 1) | (sub % 4 == 2)

    def differences(d, tiles):
        for i in range(2):
            v = tiles[i]
            at = 16 * i + d
            ff[at, 0] = v - pltpu.roll(v, 7, 0)
            ff[at, 1] = v - pltpu.roll(v, 127, 1)
            ff[at, 2] = v - pltpu.roll(v, 4, 0)
            ff[at, 3] = v

    differences(m, [pieces[q, 0], pieces[q, 1]])
    got_ints[q] = ints[...]
    got_floats[q] = floats[...]

    @pl.when(get_edge)
    def _():
        kl_copy().wait_recv()

    @pl.when(get_low)
    def _():
        cof[:, 0:1, :] = got_kl[:, 0:1, :]
        cof[:, 4:5, :] = got_kl[:, 1:2, :]

    @pl.when(get_high)
    def _():
        cof[:, 3:4, :] = got_kl[:, 0:1, :]
        cof[:, 7:8, :] = got_kl[:, 1:2, :]

    for k in range(KL):
        a = cof[k]
        aa[k, 0] = 0.5 * (a + pltpu.roll(a, 7, 0))
        aa[k, 1] = inner * (a + pltpu.roll(a, 127, 1))
        aa[k, 2] = 0.5 * (a + pltpu.roll(a, 4, 0))
        aa[k, 3] = border * a

    hear(1)
    tell(2)
    all_of(got_ints, 7, int_ss, int_rs).wait_recv()
    all_of(got_floats, 7, flo_ss, flo_rs).wait_recv()
    to_smem = [
        pltpu.make_async_copy(got_ints, int_s, smem_sem.at[0]),
        pltpu.make_async_copy(got_floats, float_s, smem_sem.at[1]),
    ]
    for copy in to_smem:
        copy.start()

    def take(i):
        main_copy(i).wait_recv()
        d = group_source(GROUP[i])
        differences(d, [got[d, 0], got[d, 1]])

    for i in range(14, 7, -1):
        take(i)
    for copy in to_smem:
        copy.wait()

    def weigh(h, carry):
        for i in range(2):
            for e in range(TERMS):
                k = int_s[h, 1, i, e]
                w = float_s[h, i, e]
                for d in range(4):
                    wa[2 * h + i, e, d] = w * aa[k, d]
        return carry

    lax.fori_loop(0, 8, weigh, 0)
    for i in range(7, -1, -1):
        take(i)

    @pl.when(get_edge)
    def _():
        all_of(got_edges, 16, edge_ss.at[0], edge_rs).wait_recv()

    @pl.when(get_low)
    def _():
        for i in range(2):
            for z in range(2):
                at = (pl.ds(16 * i, 16), 0, slice(4 * z, 4 * z + 1))
                ff[at] = ff[at] + got_edges[:, 2 * i + z : 2 * i + z + 1, :]

    @pl.when(get_high)
    def _():
        for i in range(2):
            for z in range(2):
                at = (pl.ds(16 * i, 16), 0, slice(4 * z + 2, 4 * z + 3))
                ff[at] = ff[at] - got_edges[:, 2 * i + z : 2 * i + z + 1, :]

    def four_modes(h, carry):
        norm, curve, energy = carry
        for j in range(4):
            n = 4 * h + j
            own = 16 * (j % 2) + g * 8 + 2 * h + j // 2
            flux_x = aa[0, 0] * ff[own, 0]
            flux_y = aa[0, 1] * ff[own, 1]
            rest = aa[0, 2] * ff[own, 2] + aa[0, 3] * ff[own, 3]
            for e in range(TERMS):
                p = int_s[2 * h + j // 2, 0, j % 2, e]
                flux_x += wa[n, e, 0] * ff[p, 0]
                flux_y += wa[n, e, 1] * ff[p, 1]
                rest += wa[n, e, 2] * ff[p, 2] + wa[n, e, 3] * ff[p, 3]
            out = rest + (flux_x - pltpu.roll(flux_x, 1, 0)) + (flux_y - pltpu.roll(flux_y, 1, 1))
            img[n] = out
            out = jnp.where(valid, out, 0.0)
            v = jnp.where(valid, ff[own, 3], 0.0)
            norm, curve, energy = norm + v * v, curve + v * out, energy + out * out
        return norm, curve, energy

    zero = jnp.zeros((8, 128), F32)
    parts = lax.fori_loop(0, 4, four_modes, (zero, zero, zero))

    sum_a[...] = jnp.zeros((4, 128), F32)
    for i in range(3):
        sum_a[i : i + 1, :] = jnp.sum(parts[i], axis=0, keepdims=True)

    def a_copy(t):
        return pltpu.make_async_remote_copy(
            src_ref=sum_a, dst_ref=sums_a.at[own_plane], send_sem=a_ss, recv_sem=a_rs,
            device_id=in_plane(t), device_id_type=MESH,
        )

    def b_copy(d):
        return pltpu.make_async_remote_copy(
            src_ref=sum_b, dst_ref=sums_b.at[z_at], send_sem=b_ss, recv_sem=b_rs,
            device_id=along_z(d), device_id_type=MESH,
        )

    def back_copy(t):
        return pltpu.make_async_remote_copy(
            src_ref=img.at[pl.ds(2 * row_of[t[0]][t[1]], 2)], dst_ref=back.at[q], send_sem=back_ss, recv_sem=back_rs,
            device_id=in_half(t), device_id_type=MESH,
        )

    for t in PLANE:
        a_copy(t).start()
    sums_a[own_plane] = sum_a[...]
    hear(2)
    all_of(sums_a, 31, a_ss, a_rs).wait_recv()
    sum_b[...] = jnp.sum(sums_a[...], axis=0)
    for d in RING:
        b_copy(d).start()
    for t in HALF:
        back_copy(t).start()
    sums_b[z_at] = sum_b[...]
    back[q] = img[pl.ds(2 * q, 2)]

    all_of(back, 7, back_ss, back_rs).wait_recv()
    for i in range(2):
        for z in range(2):
            for h in range(2):
                tile = pltpu.roll(back[4 * h, i], 7 - 4 * z, 0)
                for j in range(1, 4):
                    tile = jnp.where(sub // 2 == j, pltpu.roll(back[4 * h + j, i], (2 * j + 7 - 4 * z) % 8, 0), tile)
                image_ref[i, z, 8 * h : 8 * h + 8, :] = tile
    loads[5].wait()

    all_of(got, 15, main_ss, main_rs.at[0]).wait_send()
    all_of(got_ints, 7, int_ss, int_rs).wait_send()
    all_of(got_floats, 7, flo_ss, flo_rs).wait_send()
    all_of(back, 7, back_ss, back_rs).wait_send()
    all_of(sums_a, 31, a_ss, a_rs).wait_send()

    @pl.when(put_kl)
    def _():
        kl_copy().wait_send()

    @pl.when(high)
    def _():
        edge_copy(True, 0).wait_send()
        edge_copy(True, 1).wait_send()

    @pl.when(low)
    def _():
        edge_copy(False, 0).wait_send()
        edge_copy(False, 1).wait_send()

    all_of(sums_b, 15, b_ss, b_rs).wait_recv()
    sums = jnp.sum(jnp.sum(sums_b[...], axis=0), axis=1, keepdims=True)
    norm, curve, energy = sums[0:1], sums[1:2], sums[2:3]
    step = curve / (energy + EPS)
    norm_new = jnp.maximum(norm - 2.0 * step * curve + step * step * energy, 0.0)
    beta = norm_new / (norm + EPS)
    for i in range(2):
        for z in range(2):
            for h in range(2):
                rows = pl.ds(8 * h, 8)
                r = res[i, z, 8 + 8 * h : 16 + 8 * h, :]
                sol_ref[i, z, rows, :] = sol[i, z, rows, :] + step * r
                r_new = r - step * image_ref[i, z, rows, :]
                res_ref[i, z, rows, :] = r_new
                dir_ref[i, z, rows, :] = r_new + beta * r
    all_of(sums_b, 15, b_ss, b_rs).wait_send()


def deliver(*refs):
    sem = refs[8]
    copies = [pltpu.make_async_copy(refs[i], refs[4 + i], sem.at[i]) for i in range(4)]
    for copy in copies:
        copy.start()
    for copy in copies:
        copy.wait()


def on_device(residual, solution, kl_terms, partner, kl_index, coefficient):
    vmem = pl.BlockSpec(memory_space=pltpu.VMEM)
    anywhere = pl.BlockSpec(memory_space=pl.ANY)
    dma = pltpu.SemaphoreType.DMA
    field = pltpu.VMEM(residual.shape, F32)
    i32 = jnp.int32
    results = pl.pallas_call(
        galerkin,
        out_shape=(field,) * 4,
        in_specs=[anywhere] * 6,
        out_specs=(vmem,) * 4,
        scratch_shapes=[
            pltpu.VMEM((2, 2, 32, 128), F32),
            pltpu.VMEM((2, 2, 16, 128), F32),
            pltpu.VMEM((KL, 2, 32, 128), F32),
            pltpu.VMEM((2, TERMS), i32),
            pltpu.VMEM((2, TERMS), i32),
            pltpu.VMEM((2, TERMS), F32),
            pltpu.VMEM((8, 2, 8, 128), F32),
            pltpu.VMEM((2, 4, 128), F32),
            pltpu.VMEM((KL, 2, 128), F32),
            pltpu.VMEM((2, 2, 128), i32),
            pltpu.VMEM((2, 128), F32),
            pltpu.VMEM((16, 2, 8, 128), F32),
            pltpu.VMEM((16, 4, 128), F32),
            pltpu.VMEM((KL, 2, 128), F32),
            pltpu.VMEM((8, 2, 2, 128), i32),
            pltpu.VMEM((8, 2, 128), F32),
            pltpu.SMEM((8, 2, 2, 128), i32),
            pltpu.SMEM((8, 2, 128), F32),
            pltpu.VMEM((KL, 8, 128), F32),
            pltpu.VMEM((KL, 4, 8, 128), F32),
            pltpu.VMEM((16, TERMS, 4, 8, 128), F32),
            pltpu.VMEM((MODES, 4, 8, 128), F32),
            pltpu.VMEM((16, 8, 128), F32),
            pltpu.VMEM((8, 2, 8, 128), F32),
            pltpu.VMEM((4, 128), F32),
            pltpu.VMEM((32, 4, 128), F32),
            pltpu.VMEM((4, 128), F32),
            pltpu.VMEM((16, 4, 128), F32),
            dma((6,)),
            dma, dma((15,)),
            dma((4,)), dma,
            dma, dma,
            dma, dma,
            dma, dma,
            dma((2,)),
            dma, dma,
            dma, dma,
            dma, dma,
            pltpu.SemaphoreType.REGULAR((3,)),
        ],
        compiler_params=pltpu.CompilerParams(
            collective_id=0, has_side_effects=True, vmem_limit_bytes=60 << 20
        ),
        name="galerkin",
    )(residual, solution, kl_terms, partner, kl_index, coefficient)
    return pl.pallas_call(
        deliver,
        out_shape=(jax.ShapeDtypeStruct(residual.shape, F32),) * 4,
        in_specs=[vmem] * 4,
        out_specs=(anywhere,) * 4,
        scratch_shapes=[dma((4,))],
        compiler_params=pltpu.CompilerParams(vmem_limit_bytes=60 << 20),
        name="deliver",
    )(*(pltpu.with_memory_space_constraint(a, pltpu.VMEM) for a in results))


def solution(mesh):
    field = P("mode", None, "space", None)
    row = P("mode", None)
    return jax.shard_map(
        on_device,
        mesh=mesh,
        in_specs=(field, field, P(None, None, "space", None), row, row, row),
        out_specs=(field, field, field, field),
        check_vma=False,
    )
```

```python
import jax
import jax.numpy as jnp
from jax import lax
from jax.experimental import pallas as pl
from jax.experimental.pallas import tpu as pltpu
from jax.sharding import PartitionSpec as P

EPS = 1e-6
MESH = pl.DeviceIdType.MESH
KL, TERMS, MODES = 21, 24, 32
F32 = jnp.float32


def hops(dy):
    return min(dy, 4 - dy)


SHIFTS = sorted(((b, d) for b in range(4) for d in (0, 1)), key=lambda t: (-hops(t[0]), -t[1]))
RING = [8, 7, 9, 6, 10, 5, 11, 4, 12, 3, 13, 2, 14, 1, 15]


def chunk(row):
    return jnp.where(row == 0, 0, jnp.where(row == 1, 7, row - 1))


def galerkin(
    res_hbm, sol_hbm, kl_hbm, part_hbm, term_hbm, coef_hbm,
    image_ref, sol_ref, res_ref, dir_ref,
    res, sol, klv, part_v, term_v, coef_v,
    pieces, edges, kl_edge, ints, floats,
    got, got_edges, got_kl, got_ints, got_floats, int_s, float_s,
    cof, aa, wa, ff, flux, img, back, sum_a, sums_a, sum_b, sums_b,
    in_sem, main_ss, main_rs, edge_ss, edge_rs, kle_ss, kle_rs,
    int_ss, int_rs, flo_ss, flo_rs, smem_sem,
    a_ss, a_rs, b_ss, b_rs, back_ss, back_rs, ring_sem, here_sem,
):
    m, s = lax.axis_index("mode"), lax.axis_index("space")
    g, q = m // 8, chunk(m % 8)
    y, c, xl, z_at = (m // 2) % 4, m % 2, s // 16, s % 16
    ys = [(y + b) % 4 for b in range(4)]
    cs = [c, 1 - c]
    row_of = [[ys[b] * 2 + cs[d] for d in range(2)] for b in range(4)]
    across = (1 - xl) * 16 + z_at
    works, sends = g == 0, g == 1
    low, high = s > 0, s < 31
    first, last = m == 0, m == 1
    get_low, get_high = first & low, last & high
    get_edge = get_low | get_high
    put_kl = (first & high) | (last & low)
    below, above = jnp.maximum(s - 1, 0), jnp.minimum(s + 1, 31)

    loads = [
        pltpu.make_async_copy(a, b, in_sem.at[i])
        for i, (a, b) in enumerate(
            (
                (res_hbm, res.at[:, :, 8:24, :]),
                (part_hbm, part_v),
                (term_hbm, term_v),
                (coef_hbm, coef_v),
                (kl_hbm, klv.at[:, :, 8:24, :]),
                (sol_hbm, sol),
            )
        )
    ]
    for load in loads[:4]:
        load.start()

    barrier = pltpu.get_barrier_semaphore()

    def greet(device):
        pl.semaphore_signal(barrier, inc=1, device_id=device, device_id_type=MESH)

    def along_z(d):
        return m, xl * 16 + (z_at + d) % 16

    @pl.when(works)
    def _():
        for b, d in SHIFTS:
            greet((8 + row_of[b][d], s))
            greet((8 + row_of[b][d], across))
        for b, d in SHIFTS:
            greet((row_of[b][d], across))
            if b or d:
                greet((row_of[b][d], s))

    @pl.when(get_low)
    def _():
        for t in range(15, -1, -1):
            greet((t, below))

    @pl.when(get_high)
    def _():
        for t in range(15, -1, -1):
            greet((t, above))

    greet(along_z(1))
    greet(along_z(15))
    for load in loads[4:]:
        load.start()

    for i in range(2):
        for z in range(2):
            res[i, z, 0:8, :] = jnp.zeros((8, 128), F32)
            res[i, z, 24:32, :] = jnp.zeros((8, 128), F32)
    for load in loads[:4]:
        load.wait()
    ints[0, :, 0:TERMS] = (part_v[...] % 2) * 16 + part_v[...] // 2
    ints[1, :, 0:TERMS] = term_v[...]
    floats[:, 0:TERMS] = coef_v[...]
    for j in range(8):
        for i in range(2):
            for z in range(2):
                pieces[j, i, 4 * z : 4 * z + 4, :] = res[i, z, 2 * j + 7 : 2 * j + 11, :]
    for i in range(2):
        for z in range(2):
            edges[0, 2 * i + z : 2 * i + z + 1, :] = res[i, z, 23:24, :]
            edges[1, 2 * i + z : 2 * i + z + 1, :] = res[i, z, 8:9, :]

    pl.semaphore_wait(barrier, 17 + g + low.astype(jnp.int32) + high.astype(jnp.int32))

    def tell(i):
        for d in (1 << i, 16 - (1 << i)):
            pl.semaphore_signal(ring_sem.at[i], inc=1, device_id=along_z(d), device_id_type=MESH)

    def hear(i):
        pl.semaphore_wait(ring_sem.at[i], 2)

    def copy_to(src, dst, send_sem, recv_sem, device):
        return pltpu.make_async_remote_copy(
            src_ref=src, dst_ref=dst, send_sem=send_sem, recv_sem=recv_sem, device_id=device, device_id_type=MESH
        )

    def main_copy(i):
        to = row_of[SHIFTS[i][0]][SHIFTS[i][1]]
        return copy_to(pieces.at[chunk(to)], got.at[m], main_ss, main_rs.at[g * 8 + i], (to, s))

    def int_copy(i):
        return copy_to(ints, got_ints.at[m], int_ss, int_rs.at[g], (row_of[SHIFTS[i][0]][SHIFTS[i][1]], s))

    def float_copy(i):
        return copy_to(floats, got_floats.at[m], flo_ss, flo_rs.at[g], (row_of[SHIFTS[i][0]][SHIFTS[i][1]], s))

    def edge_copy(up):
        to = (0, above) if up else (1, below)
        return copy_to(edges.at[1 - up], got_edges.at[m], edge_ss.at[up], edge_rs, to)

    def kl_copy():
        return copy_to(kl_edge, got_kl, kle_ss, kle_rs, (m, jnp.where(first, above, below)))

    def all_of(ref, n, send_sem, recv_sem):
        return copy_to(ref.at[pl.ds(0, n)], ref.at[pl.ds(0, n)], send_sem, recv_sem, (m, s))

    @pl.when(high)
    def _():
        edge_copy(1).start()

    @pl.when(low)
    def _():
        edge_copy(0).start()

    for i in range(7):
        int_copy(i).start()
        float_copy(i).start()
    for i in range(7):
        main_copy(i).start()

    @pl.when(sends)
    def _():
        int_copy(7).start()
        float_copy(7).start()
        main_copy(7).start()

    tell(0)

    @pl.when(sends)
    def _():
        for t in range(8):
            for to in ((t, s), (t, across)):
                pl.semaphore_signal(here_sem, inc=1, device_id=to, device_id_type=MESH)
        hear(0)
        tell(1)
        hear(1)
        tell(2)

    lane = lax.broadcasted_iota(jnp.int32, (8, 128), 1)
    sub = lax.broadcasted_iota(jnp.int32, (8, 128), 0)
    row = sub % 4
    inner = jnp.where(lane < 127, 0.5, 0.0).astype(F32)
    border = (0.5 + jnp.where(lane == 0, 0.5, 0.0) + jnp.where(lane == 127, 0.5, 0.0)).astype(F32)
    valid = (row == 1) | (row == 2)

    def faces(x, z):
        return jnp.where(sub == 3, pltpu.roll(z, 2, 0), jnp.where(sub == 7, pltpu.roll(z, 5, 0), x))

    def rows(y, own):
        return jnp.where(row == 0, pltpu.roll(own, 7, 0), jnp.where(row == 3, pltpu.roll(own, 1, 0), y))

    def differences(d, tiles):
        for i in range(2):
            v = tiles[i]
            ff[16 * i + d, 0] = faces(v - pltpu.roll(v, 7, 0), v - pltpu.roll(v, 4, 0))
            ff[16 * i + d, 1] = rows(v - pltpu.roll(v, 127, 1), v)

    def take(a, i):
        copy_to(pieces.at[0], got.at[0], main_ss, main_rs.at[a * 8 + i], (m, s)).wait_recv()
        d = a * 8 + row_of[(4 - SHIFTS[i][0]) % 4][SHIFTS[i][1]]
        differences(d, [got[d, 0], got[d, 1]])

    def weigh(h, carry):
        for i in range(2):
            for e in range(TERMS):
                k = int_s[h, 1, i, e]
                w = float_s[h, i, e]
                wa[2 * h + i, e, 0] = w * aa[k, 0]
                wa[2 * h + i, e, 1] = w * aa[k, 1]
        return carry

    def eight_modes(h, carry):
        for j in range(8):
            n = 8 * h + j
            o, i = 4 * h + j // 2, j % 2
            one = aa[0, 0] * ff[16 * i + o, 0]
            two = aa[0, 1] * ff[16 * i + o, 1]
            for e in range(TERMS):
                p = int_s[o, 0, i, e]
                one += wa[n, e, 0] * ff[p, 0]
                two += wa[n, e, 1] * ff[p, 1]
            flux[n, 0] = one
            flux[n, 1] = two
        return carry

    row_0 = jnp.where(row == 0, 1.0, 0.0).astype(F32)
    row_2 = jnp.where(row == 2, 1.0, 0.0).astype(F32)
    last_sub = jnp.where(sub == 7, 1.0, 0.0).astype(F32)

    def sixteen_modes(h, carry):
        norm, curve, energy = carry
        for j in range(16):
            n = 16 * h + j
            one, two = flux[n, 0], flux[n, 1]
            out = one + two - pltpu.roll(two, 1, 1)
            out += pltpu.roll(row_0 * two - one, 1, 0)
            out += row_2 * pltpu.roll(two - last_sub * one, 7, 0)
            out += jnp.where(sub == 1, pltpu.roll(one, 6, 0), jnp.where(sub == 2, pltpu.roll(one, 3, 0), 0.0))
            out -= jnp.where(sub == 5, pltpu.roll(one, 2, 0), 0.0)
            img[n] = out
            out = jnp.where(valid, out, 0.0)
            v = jnp.where(valid, got[8 * h + j // 2, j % 2], 0.0)
            norm, curve, energy = norm + v * v, curve + v * out, energy + out * out
        return norm, curve, energy

    own_sum = xl * 8 + m % 8

    def a_copy(mode, space):
        return copy_to(sum_a, sums_a.at[own_sum], a_ss, a_rs, (mode, space))

    def to_scalars(a):
        half = pl.ds(8 * a, 8)
        copies = [
            pltpu.make_async_copy(got_ints.at[half], int_s.at[half], smem_sem.at[2 * a]),
            pltpu.make_async_copy(got_floats.at[half], float_s.at[half], smem_sem.at[2 * a + 1]),
        ]
        for copy in copies:
            copy.start()
        return copies

    @pl.when(works)
    def _():
        loads[4].wait()
        end = jnp.where(first, 23, 8)
        for z in range(2):
            kl_edge[:, z : z + 1, :] = klv[:, z, pl.ds(end, 1), :]

        @pl.when(put_kl)
        def _():
            kl_copy().start()

        got_ints[m] = ints[...]
        got_floats[m] = floats[...]
        hear(0)
        tell(1)

        for z in range(2):
            for r in range(4):
                cof[:, 4 * z + r : 4 * z + r + 1, :] = klv[:, z, pl.ds(2 * q + 7 + r, 1), :]

        @pl.when(first)
        def _():
            cof[:, 0:1, :] = jnp.zeros((KL, 1, 128), F32)
            cof[:, 4:5, :] = jnp.zeros((KL, 1, 128), F32)

        @pl.when(last)
        def _():
            cof[:, 3:4, :] = jnp.zeros((KL, 1, 128), F32)
            cof[:, 7:8, :] = jnp.zeros((KL, 1, 128), F32)

        got[m] = pieces[q]
        differences(m, [pieces[q, 0], pieces[q, 1]])

        @pl.when(get_edge)
        def _():
            kl_copy().wait_recv()

        @pl.when(get_low)
        def _():
            cof[:, 0:1, :] = got_kl[:, 0:1, :]
            cof[:, 4:5, :] = got_kl[:, 1:2, :]

        @pl.when(get_high)
        def _():
            cof[:, 3:4, :] = got_kl[:, 0:1, :]
            cof[:, 7:8, :] = got_kl[:, 1:2, :]

        for k in range(KL):
            a = cof[k]
            aa[k, 0] = faces(0.5 * (a + pltpu.roll(a, 7, 0)), 0.5 * (a + pltpu.roll(a, 4, 0)))
            aa[k, 1] = rows(inner * (a + pltpu.roll(a, 127, 1)), border * a)

        hear(1)
        tell(2)
        all_of(got_ints, 7, int_ss, int_rs.at[0]).wait_recv()
        all_of(got_floats, 7, flo_ss, flo_rs.at[0]).wait_recv()
        near = to_scalars(0)
        for i in range(6, -1, -1):
            take(0, i)
        for copy in near:
            copy.wait()
        lax.fori_loop(0, 8, weigh, 0)
        all_of(got_ints, 8, int_ss, int_rs.at[1]).wait_recv()
        all_of(got_floats, 8, flo_ss, flo_rs.at[1]).wait_recv()
        far = to_scalars(1)
        for i in range(7, -1, -1):
            take(1, i)

        @pl.when(get_edge)
        def _():
            all_of(got_edges, 16, edge_ss.at[0], edge_rs).wait_recv()

        @pl.when(get_low)
        def _():
            for i in range(2):
                for z in range(2):
                    at = (pl.ds(16 * i, 16), 0, slice(4 * z, 4 * z + 1))
                    ff[at] = ff[at] + got_edges[:, 2 * i + z : 2 * i + z + 1, :]

        @pl.when(get_high)
        def _():
            for i in range(2):
                for z in range(2):
                    at = (pl.ds(16 * i, 16), 0, slice(4 * z + 2, 4 * z + 3))
                    ff[at] = ff[at] - got_edges[:, 2 * i + z : 2 * i + z + 1, :]

        zero = jnp.zeros((8, 128), F32)
        lax.fori_loop(0, 2, eight_modes, 0)
        for copy in far:
            copy.wait()
        lax.fori_loop(8, 16, weigh, 0)
        lax.fori_loop(2, 4, eight_modes, 0)
        parts = lax.fori_loop(0, 2, sixteen_modes, (zero, zero, zero))

        sum_a[...] = jnp.zeros((4, 128), F32)
        for i in range(3):
            sum_a[i : i + 1, :] = jnp.sum(parts[i], axis=0, keepdims=True)
        pl.semaphore_wait(here_sem, 16)
        for half in (0, 8):
            for b, d in SHIFTS:
                a_copy(half + row_of[b][d], across).start()
                if half or b or d:
                    a_copy(half + row_of[b][d], s).start()
        sums_a[own_sum] = sum_a[...]
        all_of(sums_a, 15, a_ss, a_rs).wait_recv()

    @pl.when(sends)
    def _():
        all_of(sums_a, 16, a_ss, a_rs).wait_recv()

    def b_copy(d):
        return copy_to(sum_b, sums_b.at[z_at], b_ss, b_rs, along_z(d))

    def back_copy(to):
        return copy_to(img.at[pl.ds(2 * to, 2)], back.at[q], back_ss, back_rs, (to, s))

    sum_b[...] = jnp.sum(sums_a[...], axis=0)
    hear(2)
    for d in RING:
        b_copy(d).start()
    sums_b[z_at] = sum_b[...]

    @pl.when(works)
    def _():
        for b, d in SHIFTS:
            back_copy(8 + row_of[b][d]).start()
            if b or d:
                back_copy(row_of[b][d]).start()
        back[q] = img[pl.ds(2 * m, 2)]
        all_of(back, 7, back_ss, back_rs).wait_recv()

    @pl.when(sends)
    def _():
        all_of(back, 8, back_ss, back_rs).wait_recv()

    for i in range(2):
        for z in range(2):
            for h in range(2):
                tile = pltpu.roll(back[4 * h, i], 7 - 4 * z, 0)
                for j in range(1, 4):
                    tile = jnp.where(sub // 2 == j, pltpu.roll(back[4 * h + j, i], (2 * j + 7 - 4 * z) % 8, 0), tile)
                image_ref[i, z, 8 * h : 8 * h + 8, :] = tile
    loads[5].wait()

    @pl.when(works)
    def _():
        all_of(pieces, 7, main_ss, main_rs.at[0]).wait_send()
        all_of(got_ints, 7, int_ss, int_rs.at[0]).wait_send()
        all_of(got_floats, 7, flo_ss, flo_rs.at[0]).wait_send()
        all_of(got, 15, back_ss, back_rs).wait_send()
        all_of(sums_b, 16, a_ss, a_rs).wait_send()
        all_of(sums_b, 15, a_ss, a_rs).wait_send()

    @pl.when(sends)
    def _():
        loads[4].wait()
        all_of(pieces, 8, main_ss, main_rs.at[0]).wait_send()
        all_of(got_ints, 8, int_ss, int_rs.at[0]).wait_send()
        all_of(got_floats, 8, flo_ss, flo_rs.at[0]).wait_send()

    @pl.when(put_kl)
    def _():
        kl_copy().wait_send()

    @pl.when(high)
    def _():
        edge_copy(1).wait_send()

    @pl.when(low)
    def _():
        edge_copy(0).wait_send()

    all_of(sums_b, 15, b_ss, b_rs).wait_recv()
    sums = jnp.sum(jnp.sum(sums_b[...], axis=0), axis=1, keepdims=True)
    norm, curve, energy = sums[0:1], sums[1:2], sums[2:3]
    step = curve / (energy + EPS)
    norm_new = jnp.maximum(norm - 2.0 * step * curve + step * step * energy, 0.0)
    beta = norm_new / (norm + EPS)
    for i in range(2):
        for z in range(2):
            for h in range(2):
                at = pl.ds(8 * h, 8)
                r = res[i, z, 8 + 8 * h : 16 + 8 * h, :]
                sol_ref[i, z, at, :] = sol[i, z, at, :] + step * r
                r_new = r - step * image_ref[i, z, at, :]
                res_ref[i, z, at, :] = r_new
                dir_ref[i, z, at, :] = r_new + beta * r
    all_of(sums_b, 15, b_ss, b_rs).wait_send()


def deliver(*refs):
    sem = refs[8]
    copies = [pltpu.make_async_copy(refs[i], refs[4 + i], sem.at[i]) for i in range(4)]
    for copy in copies:
        copy.start()
    for copy in copies:
        copy.wait()


def on_device(residual, solution, kl_terms, partner, kl_index, coefficient):
    vmem = pl.BlockSpec(memory_space=pltpu.VMEM)
    anywhere = pl.BlockSpec(memory_space=pl.ANY)
    dma = pltpu.SemaphoreType.DMA
    field = pltpu.VMEM(residual.shape, F32)
    i32 = jnp.int32
    results = pl.pallas_call(
        galerkin,
        out_shape=(field,) * 4,
        in_specs=[anywhere] * 6,
        out_specs=(vmem,) * 4,
        scratch_shapes=[
            pltpu.VMEM((2, 2, 32, 128), F32),
            pltpu.VMEM((2, 2, 16, 128), F32),
            pltpu.VMEM((KL, 2, 32, 128), F32),
            pltpu.VMEM((2, TERMS), i32),
            pltpu.VMEM((2, TERMS), i32),
            pltpu.VMEM((2, TERMS), F32),
            pltpu.VMEM((8, 2, 8, 128), F32),
            pltpu.VMEM((2, 4, 128), F32),
            pltpu.VMEM((KL, 2, 128), F32),
            pltpu.VMEM((2, 2, 128), i32),
            pltpu.VMEM((2, 128), F32),
            pltpu.VMEM((16, 2, 8, 128), F32),
            pltpu.VMEM((16, 4, 128), F32),
            pltpu.VMEM((KL, 2, 128), F32),
            pltpu.VMEM((16, 2, 2, 128), i32),
            pltpu.VMEM((16, 2, 128), F32),
            pltpu.SMEM((16, 2, 2, 128), i32),
            pltpu.SMEM((16, 2, 128), F32),
            pltpu.VMEM((KL, 8, 128), F32),
            pltpu.VMEM((KL, 2, 8, 128), F32),
            pltpu.VMEM((MODES, TERMS, 2, 8, 128), F32),
            pltpu.VMEM((MODES, 2, 8, 128), F32),
            pltpu.VMEM((MODES, 2, 8, 128), F32),
            pltpu.VMEM((MODES, 8, 128), F32),
            pltpu.VMEM((8, 2, 8, 128), F32),
            pltpu.VMEM((4, 128), F32),
            pltpu.VMEM((16, 4, 128), F32),
            pltpu.VMEM((4, 128), F32),
            pltpu.VMEM((16, 4, 128), F32),
            dma((6,)),
            dma, dma((16,)),
            dma((2,)), dma,
            dma, dma,
            dma, dma((2,)),
            dma, dma((2,)),
            dma((4,)),
            dma, dma,
            dma, dma,
            dma, dma,
            pltpu.SemaphoreType.REGULAR((3,)),
            pltpu.SemaphoreType.REGULAR,
        ],
        compiler_params=pltpu.CompilerParams(
            collective_id=0, has_side_effects=True, vmem_limit_bytes=60 << 20
        ),
        name="galerkin",
    )(residual, solution, kl_terms, partner, kl_index, coefficient)
    return pl.pallas_call(
        deliver,
        out_shape=(jax.ShapeDtypeStruct(residual.shape, F32),) * 4,
        in_specs=[vmem] * 4,
        out_specs=(anywhere,) * 4,
        scratch_shapes=[dma((4,))],
        compiler_params=pltpu.CompilerParams(vmem_limit_bytes=60 << 20),
        name="deliver",
    )(*(pltpu.with_memory_space_constraint(a, pltpu.VMEM) for a in results))


def solution(mesh):
    field = P("mode", None, "space", None)
    row = P("mode", None)
    return jax.shard_map(
        on_device,
        mesh=mesh,
        in_specs=(field, field, P(None, None, "space", None), row, row, row),
        out_specs=(field, field, field, field),
        check_vma=False,
    )
```

```python
import jax
import jax.numpy as jnp
from jax import lax
from jax.experimental import pallas as pl
from jax.experimental.pallas import tpu as pltpu
from jax.sharding import PartitionSpec as P

EPS = 1e-6
MESH = pl.DeviceIdType.MESH
KL, TERMS, MODES = 21, 24, 32
F32 = jnp.float32


FLIPS = [(a, b, d) for a in (1, 0) for b in (1, 0) for d in (1, 0)]
RING = [8, 7, 9, 6, 10, 5, 11, 4, 12, 3, 13, 2, 14, 1, 15]


def chunk(r):
    return jnp.where(r == 0, 0, jnp.where(r == 1, 7, r - 1))


def galerkin(
    res_hbm, sol_hbm, kl_hbm, part_hbm, term_hbm, coef_hbm,
    image_ref, sol_ref, res_ref, dir_ref,
    res, sol, klv, part_v, term_v, coef_v,
    pieces, edges, kl_edge, ints, floats,
    got, got_edges, got_kl, got_ints, got_floats, int_s, float_s,
    cof, aa, wa, ff, flux, img, back, sum_a, sums_a, sum_b, sums_b,
    in_sem, main_ss, main_rs, edge_ss, edge_rs, kle_ss, kle_rs,
    int_ss, int_rs, flo_ss, flo_rs, smem_sem,
    a_ss, a_rs, b_ss, b_rs, back_ss, back_rs, ring_sem, here_sem,
):
    m, s = lax.axis_index("mode"), lax.axis_index("space")
    xh, y, c, xl, z_at = m // 8, (m // 2) % 4, m % 2, s // 16, s % 16
    g, yb = y // 2, y % 2
    r = xh * 4 + yb * 2 + c
    slot, q = g * 8 + r, chunk(r)
    r_of = {f: (1 - xh if f[0] else xh) * 4 + (1 - yb if f[1] else yb) * 2 + (1 - c if f[2] else c) for f in FLIPS}
    mode_of = {f: (1 - xh if f[0] else xh) * 8 + (1 - yb if f[1] else yb) * 2 + (1 - c if f[2] else c) for f in FLIPS}
    SELF = FLIPS[7]
    across = (1 - xl) * 16 + z_at
    works, sends = g == 0, g == 1
    low, high = s > 0, s < 31
    first, last = m == 0, m == 1
    get_low, get_high = first & low, last & high
    get_edge = get_low | get_high
    put_kl = (first & high) | (last & low)
    below, above = jnp.maximum(s - 1, 0), jnp.minimum(s + 1, 31)

    loads = [
        pltpu.make_async_copy(a, b, in_sem.at[i])
        for i, (a, b) in enumerate(
            (
                (res_hbm, res.at[:, :, 8:24, :]),
                (part_hbm, part_v),
                (term_hbm, term_v),
                (coef_hbm, coef_v),
                (kl_hbm, klv.at[:, :, 8:24, :]),
                (sol_hbm, sol),
            )
        )
    ]
    for load in loads[:4]:
        load.start()

    barrier = pltpu.get_barrier_semaphore()

    def greet(device):
        pl.semaphore_signal(barrier, inc=1, device_id=device, device_id_type=MESH)

    def along_z(d):
        return m, xl * 16 + (z_at + d) % 16

    @pl.when(works)
    def _():
        for f in FLIPS:
            greet((mode_of[f] + 4, s))
            greet((mode_of[f] + 4, across))
        for f in FLIPS:
            greet((mode_of[f], across))
            if f != SELF:
                greet((mode_of[f], s))

    @pl.when(get_low)
    def _():
        for t in range(15, -1, -1):
            greet((t, below))

    @pl.when(get_high)
    def _():
        for t in range(15, -1, -1):
            greet((t, above))

    greet(along_z(1))
    greet(along_z(15))
    for load in loads[4:]:
        load.start()

    for i in range(2):
        for z in range(2):
            res[i, z, 0:8, :] = jnp.zeros((8, 128), F32)
            res[i, z, 24:32, :] = jnp.zeros((8, 128), F32)
    for load in loads[:4]:
        load.wait()
    p = part_v[...]
    ints[0, :, 0:TERMS] = (p % 2) * 16 + (p // 8) % 2 * 8 + p // 16 * 4 + p // 2 % 4
    ints[1, :, 0:TERMS] = term_v[...]
    floats[:, 0:TERMS] = coef_v[...]
    for j in range(8):
        for i in range(2):
            for z in range(2):
                pieces[j, i, 4 * z : 4 * z + 4, :] = res[i, z, 2 * j + 7 : 2 * j + 11, :]
    for i in range(2):
        for z in range(2):
            edges[0, 2 * i + z : 2 * i + z + 1, :] = res[i, z, 23:24, :]
            edges[1, 2 * i + z : 2 * i + z + 1, :] = res[i, z, 8:9, :]

    pl.semaphore_wait(barrier, 17 + g + low.astype(jnp.int32) + high.astype(jnp.int32))

    def tell(i):
        for d in (1 << i, 16 - (1 << i)):
            pl.semaphore_signal(ring_sem.at[i], inc=1, device_id=along_z(d), device_id_type=MESH)

    def hear(i):
        pl.semaphore_wait(ring_sem.at[i], 2)

    def copy_to(src, dst, send_sem, recv_sem, device):
        return pltpu.make_async_remote_copy(
            src_ref=src, dst_ref=dst, send_sem=send_sem, recv_sem=recv_sem, device_id=device, device_id_type=MESH
        )

    def main_copy(i):
        f = FLIPS[i]
        return copy_to(pieces.at[chunk(r_of[f])], got.at[slot], main_ss, main_rs.at[g * 8 + i], (mode_of[f], s))

    def int_copy(i):
        return copy_to(ints, got_ints.at[slot], int_ss, int_rs.at[g], (mode_of[FLIPS[i]], s))

    def float_copy(i):
        return copy_to(floats, got_floats.at[slot], flo_ss, flo_rs.at[g], (mode_of[FLIPS[i]], s))

    def edge_copy(up):
        to = (0, above) if up else (1, below)
        return copy_to(edges.at[1 - up], got_edges.at[slot], edge_ss.at[up], edge_rs, to)

    def kl_copy():
        return copy_to(kl_edge, got_kl, kle_ss, kle_rs, (m, jnp.where(first, above, below)))

    def all_of(ref, n, send_sem, recv_sem):
        return copy_to(ref.at[pl.ds(0, n)], ref.at[pl.ds(0, n)], send_sem, recv_sem, (m, s))

    @pl.when(high)
    def _():
        edge_copy(1).start()

    @pl.when(low)
    def _():
        edge_copy(0).start()

    for i in range(7):
        int_copy(i).start()
        float_copy(i).start()
    for i in range(7):
        main_copy(i).start()

    @pl.when(sends)
    def _():
        int_copy(7).start()
        float_copy(7).start()
        main_copy(7).start()

    tell(0)

    @pl.when(sends)
    def _():
        for t in (0, 1, 2, 3, 8, 9, 10, 11):
            for to in ((t, s), (t, across)):
                pl.semaphore_signal(here_sem, inc=1, device_id=to, device_id_type=MESH)
        hear(0)
        tell(1)
        hear(1)
        tell(2)

    lane = lax.broadcasted_iota(jnp.int32, (8, 128), 1)
    sub = lax.broadcasted_iota(jnp.int32, (8, 128), 0)
    row = sub % 4
    inner = jnp.where(lane < 127, 0.5, 0.0).astype(F32)
    border = (0.5 + jnp.where(lane == 0, 0.5, 0.0) + jnp.where(lane == 127, 0.5, 0.0)).astype(F32)
    valid = (row == 1) | (row == 2)

    def faces(x, z):
        return jnp.where(sub == 3, pltpu.roll(z, 2, 0), jnp.where(sub == 7, pltpu.roll(z, 5, 0), x))

    def rows(y, own):
        return jnp.where(row == 0, pltpu.roll(own, 7, 0), jnp.where(row == 3, pltpu.roll(own, 1, 0), y))

    def differences(d, tiles):
        for i in range(2):
            v = tiles[i]
            ff[16 * i + d, 0] = faces(v - pltpu.roll(v, 7, 0), v - pltpu.roll(v, 4, 0))
            ff[16 * i + d, 1] = rows(v - pltpu.roll(v, 127, 1), v)

    def take(a, places):
        for i in places:
            copy_to(pieces.at[0], got.at[0], main_ss, main_rs.at[a * 8 + i], (m, s)).wait_recv()
        for i in places:
            d = a * 8 + r_of[FLIPS[i]]
            differences(d, [got[d, 0], got[d, 1]])

    def weigh(h, carry):
        for i in range(2):
            for e in range(TERMS):
                k = int_s[h, 1, i, e]
                w = float_s[h, i, e]
                wa[2 * h + i, e, 0] = w * aa[k, 0]
                wa[2 * h + i, e, 1] = w * aa[k, 1]
        return carry

    def eight_modes(h, carry):
        for j in range(8):
            n = 8 * h + j
            o, i = 4 * h + j // 2, j % 2
            one = aa[0, 0] * ff[16 * i + o, 0]
            two = aa[0, 1] * ff[16 * i + o, 1]
            for e in range(TERMS):
                p = int_s[o, 0, i, e]
                one += wa[n, e, 0] * ff[p, 0]
                two += wa[n, e, 1] * ff[p, 1]
            flux[n, 0] = one
            flux[n, 1] = two
        return carry

    def eight_far_modes(h, carry):
        for j in range(8):
            n = 8 * h + j
            o, i = 4 * h + j // 2, j % 2
            one = aa[0, 0] * ff[16 * i + o, 0]
            two = aa[0, 1] * ff[16 * i + o, 1]
            for e in range(TERMS):
                p = int_s[o, 0, i, e]
                k = int_s[o, 1, i, e]
                w = float_s[o, i, e]
                one += w * (aa[k, 0] * ff[p, 0])
                two += w * (aa[k, 1] * ff[p, 1])
            flux[n, 0] = one
            flux[n, 1] = two
        return carry

    row_0 = jnp.where(row == 0, 1.0, 0.0).astype(F32)
    row_2 = jnp.where(row == 2, 1.0, 0.0).astype(F32)
    last_sub = jnp.where(sub == 7, 1.0, 0.0).astype(F32)

    def sixteen_modes(h, carry):
        norm, curve, energy = carry
        for j in range(16):
            n = 16 * h + j
            one, two = flux[n, 0], flux[n, 1]
            out = one + two - pltpu.roll(two, 1, 1)
            out += pltpu.roll(row_0 * two - one, 1, 0)
            out += row_2 * pltpu.roll(two - last_sub * one, 7, 0)
            out += jnp.where(sub == 1, pltpu.roll(one, 6, 0), jnp.where(sub == 2, pltpu.roll(one, 3, 0), 0.0))
            out -= jnp.where(sub == 5, pltpu.roll(one, 2, 0), 0.0)
            img[n] = out
            out = jnp.where(valid, out, 0.0)
            v = jnp.where(valid, got[8 * h + j // 2, j % 2], 0.0)
            norm, curve, energy = norm + v * v, curve + v * out, energy + out * out
        return norm, curve, energy

    own_sum = xl * 8 + r

    def a_copy(mode, space):
        return copy_to(sum_a, sums_a.at[own_sum], a_ss, a_rs, (mode, space))

    def to_scalars(a):
        half = pl.ds(8 * a, 8)
        copies = [
            pltpu.make_async_copy(got_ints.at[half], int_s.at[half], smem_sem.at[2 * a]),
            pltpu.make_async_copy(got_floats.at[half], float_s.at[half], smem_sem.at[2 * a + 1]),
        ]
        for copy in copies:
            copy.start()
        return copies

    @pl.when(works)
    def _():
        loads[4].wait()
        end = jnp.where(first, 23, 8)
        for z in range(2):
            kl_edge[:, z : z + 1, :] = klv[:, z, pl.ds(end, 1), :]

        @pl.when(put_kl)
        def _():
            kl_copy().start()

        got_ints[slot] = ints[...]
        got_floats[slot] = floats[...]
        hear(0)
        tell(1)

        for z in range(2):
            for r in range(4):
                cof[:, 4 * z + r : 4 * z + r + 1, :] = klv[:, z, pl.ds(2 * q + 7 + r, 1), :]

        @pl.when(first)
        def _():
            cof[:, 0:1, :] = jnp.zeros((KL, 1, 128), F32)
            cof[:, 4:5, :] = jnp.zeros((KL, 1, 128), F32)

        @pl.when(last)
        def _():
            cof[:, 3:4, :] = jnp.zeros((KL, 1, 128), F32)
            cof[:, 7:8, :] = jnp.zeros((KL, 1, 128), F32)

        got[slot] = pieces[q]
        differences(slot, [pieces[q, 0], pieces[q, 1]])

        @pl.when(get_edge)
        def _():
            kl_copy().wait_recv()

        @pl.when(get_low)
        def _():
            cof[:, 0:1, :] = got_kl[:, 0:1, :]
            cof[:, 4:5, :] = got_kl[:, 1:2, :]

        @pl.when(get_high)
        def _():
            cof[:, 3:4, :] = got_kl[:, 0:1, :]
            cof[:, 7:8, :] = got_kl[:, 1:2, :]

        for k in range(KL):
            a = cof[k]
            aa[k, 0] = faces(0.5 * (a + pltpu.roll(a, 7, 0)), 0.5 * (a + pltpu.roll(a, 4, 0)))
            aa[k, 1] = rows(inner * (a + pltpu.roll(a, 127, 1)), border * a)

        hear(1)
        tell(2)
        all_of(got_ints, 7, int_ss, int_rs.at[0]).wait_recv()
        all_of(got_floats, 7, flo_ss, flo_rs.at[0]).wait_recv()
        near = to_scalars(0)
        take(0, range(6, -1, -1))
        for copy in near:
            copy.wait()
        lax.fori_loop(0, 8, weigh, 0)
        all_of(got_ints, 8, int_ss, int_rs.at[1]).wait_recv()
        all_of(got_floats, 8, flo_ss, flo_rs.at[1]).wait_recv()
        far = to_scalars(1)
        take(1, range(7, -1, -1))

        @pl.when(get_edge)
        def _():
            all_of(got_edges, 16, edge_ss.at[0], edge_rs).wait_recv()

        @pl.when(get_low)
        def _():
            for i in range(2):
                for z in range(2):
                    at = (pl.ds(16 * i, 16), 0, slice(4 * z, 4 * z + 1))
                    ff[at] = ff[at] + got_edges[:, 2 * i + z : 2 * i + z + 1, :]

        @pl.when(get_high)
        def _():
            for i in range(2):
                for z in range(2):
                    at = (pl.ds(16 * i, 16), 0, slice(4 * z + 2, 4 * z + 3))
                    ff[at] = ff[at] - got_edges[:, 2 * i + z : 2 * i + z + 1, :]

        zero = jnp.zeros((8, 128), F32)
        lax.fori_loop(0, 2, eight_modes, 0)
        for copy in far:
            copy.wait()
        lax.fori_loop(2, 4, eight_far_modes, 0)
        parts = lax.fori_loop(0, 2, sixteen_modes, (zero, zero, zero))

        sum_a[...] = jnp.zeros((4, 128), F32)
        for i in range(3):
            sum_a[i : i + 1, :] = jnp.sum(parts[i], axis=0, keepdims=True)
        pl.semaphore_wait(here_sem, 16)
        for other in (0, 4):
            for f in FLIPS:
                a_copy(mode_of[f] + other, across).start()
                if other or f != SELF:
                    a_copy(mode_of[f] + other, s).start()
        sums_a[own_sum] = sum_a[...]
        all_of(sums_a, 15, a_ss, a_rs).wait_recv()

    @pl.when(sends)
    def _():
        all_of(sums_a, 16, a_ss, a_rs).wait_recv()

    def b_copy(d):
        return copy_to(sum_b, sums_b.at[z_at], b_ss, b_rs, along_z(d))

    def back_copy(f, other):
        src = img.at[pl.ds(2 * (r_of[f] + 2 * other), 2)]
        return copy_to(src, back.at[q], back_ss, back_rs, (mode_of[f] + other, s))

    sum_b[...] = jnp.sum(sums_a[...], axis=0)
    hear(2)
    for d in RING:
        b_copy(d).start()
    sums_b[z_at] = sum_b[...]

    @pl.when(works)
    def _():
        for f in FLIPS:
            back_copy(f, 4).start()
            if f != SELF:
                back_copy(f, 0).start()
        back[q] = img[pl.ds(2 * slot, 2)]
        all_of(back, 7, back_ss, back_rs).wait_recv()

    @pl.when(sends)
    def _():
        all_of(back, 8, back_ss, back_rs).wait_recv()

    for i in range(2):
        for z in range(2):
            for h in range(2):
                tile = pltpu.roll(back[4 * h, i], 7 - 4 * z, 0)
                for j in range(1, 4):
                    tile = jnp.where(sub // 2 == j, pltpu.roll(back[4 * h + j, i], (2 * j + 7 - 4 * z) % 8, 0), tile)
                image_ref[i, z, 8 * h : 8 * h + 8, :] = tile
    loads[5].wait()

    @pl.when(works)
    def _():
        all_of(pieces, 7, main_ss, main_rs.at[0]).wait_send()
        all_of(got_ints, 7, int_ss, int_rs.at[0]).wait_send()
        all_of(got_floats, 7, flo_ss, flo_rs.at[0]).wait_send()
        all_of(got, 15, back_ss, back_rs).wait_send()
        all_of(sums_b, 16, a_ss, a_rs).wait_send()
        all_of(sums_b, 15, a_ss, a_rs).wait_send()

    @pl.when(sends)
    def _():
        loads[4].wait()
        all_of(pieces, 8, main_ss, main_rs.at[0]).wait_send()
        all_of(got_ints, 8, int_ss, int_rs.at[0]).wait_send()
        all_of(got_floats, 8, flo_ss, flo_rs.at[0]).wait_send()

    @pl.when(put_kl)
    def _():
        kl_copy().wait_send()

    @pl.when(high)
    def _():
        edge_copy(1).wait_send()

    @pl.when(low)
    def _():
        edge_copy(0).wait_send()

    all_of(sums_b, 15, b_ss, b_rs).wait_recv()
    sums = jnp.sum(jnp.sum(sums_b[...], axis=0), axis=1, keepdims=True)
    norm, curve, energy = sums[0:1], sums[1:2], sums[2:3]
    step = curve / (energy + EPS)
    norm_new = jnp.maximum(norm - 2.0 * step * curve + step * step * energy, 0.0)
    beta = norm_new / (norm + EPS)
    for i in range(2):
        for z in range(2):
            for h in range(2):
                at = pl.ds(8 * h, 8)
                old = res[i, z, 8 + 8 * h : 16 + 8 * h, :]
                sol_ref[i, z, at, :] = sol[i, z, at, :] + step * old
                new = old - step * image_ref[i, z, at, :]
                res_ref[i, z, at, :] = new
                dir_ref[i, z, at, :] = new + beta * old
    all_of(sums_b, 15, b_ss, b_rs).wait_send()


def deliver(*refs):
    sem = refs[8]
    copies = [pltpu.make_async_copy(refs[i], refs[4 + i], sem.at[i]) for i in range(4)]
    for copy in copies:
        copy.start()
    for copy in copies:
        copy.wait()


def on_device(residual, solution, kl_terms, partner, kl_index, coefficient):
    vmem = pl.BlockSpec(memory_space=pltpu.VMEM)
    anywhere = pl.BlockSpec(memory_space=pl.ANY)
    dma = pltpu.SemaphoreType.DMA
    field = pltpu.VMEM(residual.shape, F32)
    i32 = jnp.int32
    results = pl.pallas_call(
        galerkin,
        out_shape=(field,) * 4,
        in_specs=[anywhere] * 6,
        out_specs=(vmem,) * 4,
        scratch_shapes=[
            pltpu.VMEM((2, 2, 32, 128), F32),
            pltpu.VMEM((2, 2, 16, 128), F32),
            pltpu.VMEM((KL, 2, 32, 128), F32),
            pltpu.VMEM((2, TERMS), i32),
            pltpu.VMEM((2, TERMS), i32),
            pltpu.VMEM((2, TERMS), F32),
            pltpu.VMEM((8, 2, 8, 128), F32),
            pltpu.VMEM((2, 4, 128), F32),
            pltpu.VMEM((KL, 2, 128), F32),
            pltpu.VMEM((2, 2, 128), i32),
            pltpu.VMEM((2, 128), F32),
            pltpu.VMEM((16, 2, 8, 128), F32),
            pltpu.VMEM((16, 4, 128), F32),
            pltpu.VMEM((KL, 2, 128), F32),
            pltpu.VMEM((16, 2, 2, 128), i32),
            pltpu.VMEM((16, 2, 128), F32),
            pltpu.SMEM((16, 2, 2, 128), i32),
            pltpu.SMEM((16, 2, 128), F32),
            pltpu.VMEM((KL, 8, 128), F32),
            pltpu.VMEM((KL, 2, 8, 128), F32),
            pltpu.VMEM((MODES // 2, TERMS, 2, 8, 128), F32),
            pltpu.VMEM((MODES, 2, 8, 128), F32),
            pltpu.VMEM((MODES, 2, 8, 128), F32),
            pltpu.VMEM((MODES, 8, 128), F32),
            pltpu.VMEM((8, 2, 8, 128), F32),
            pltpu.VMEM((4, 128), F32),
            pltpu.VMEM((16, 4, 128), F32),
            pltpu.VMEM((4, 128), F32),
            pltpu.VMEM((16, 4, 128), F32),
            dma((6,)),
            dma, dma((16,)),
            dma((2,)), dma,
            dma, dma,
            dma, dma((2,)),
            dma, dma((2,)),
            dma((4,)),
            dma, dma,
            dma, dma,
            dma, dma,
            pltpu.SemaphoreType.REGULAR((3,)),
            pltpu.SemaphoreType.REGULAR,
        ],
        compiler_params=pltpu.CompilerParams(
            collective_id=0, has_side_effects=True, vmem_limit_bytes=60 << 20
        ),
        name="galerkin",
    )(residual, solution, kl_terms, partner, kl_index, coefficient)
    return pl.pallas_call(
        deliver,
        out_shape=(jax.ShapeDtypeStruct(residual.shape, F32),) * 4,
        in_specs=[vmem] * 4,
        out_specs=(anywhere,) * 4,
        scratch_shapes=[dma((4,))],
        compiler_params=pltpu.CompilerParams(vmem_limit_bytes=60 << 20),
        name="deliver",
    )(*(pltpu.with_memory_space_constraint(a, pltpu.VMEM) for a in results))


def solution(mesh):
    field = P("mode", None, "space", None)
    row = P("mode", None)
    return jax.shard_map(
        on_device,
        mesh=mesh,
        in_specs=(field, field, P(None, None, "space", None), row, row, row),
        out_specs=(field, field, field, field),
        check_vma=False,
    )
```

```python
import jax
import jax.numpy as jnp
from jax import lax
from jax.experimental import pallas as pl
from jax.experimental.pallas import tpu as pltpu
from jax.sharding import PartitionSpec as P

EPS = 1e-6
MESH = pl.DeviceIdType.MESH
KL, TERMS, MODES = 21, 24, 32
F32 = jnp.float32


FLIPS = [(a, b, d) for a in (1, 0) for b in ((0, 1) if a else (1, 0)) for d in (1, 0)]
RING = [8, 7, 9, 6, 10, 5, 11, 4, 12, 3, 13, 2, 14, 1, 15]


def chunk(r):
    return jnp.where(r == 0, 0, jnp.where(r == 1, 7, r - 1))


def galerkin(
    res_hbm, sol_hbm, kl_hbm, part_hbm, term_hbm, coef_hbm,
    image_ref, sol_ref, res_ref, dir_ref,
    res, sol, klv, part_v, term_v, coef_v,
    pieces, edges, kl_edge, ints, floats,
    got, got_edges, got_kl, got_ints, got_floats, int_s, float_s,
    cof, aa, wa, ff, flux, img, back, sum_a, sums_a, sum_b, sums_b,
    in_sem, main_ss, main_rs, edge_ss, edge_rs, kle_ss, kle_rs,
    int_ss, int_rs, flo_ss, flo_rs, smem_sem,
    a_ss, a_rs, b_ss, b_rs, back_ss, back_rs, ring_sem, here_sem,
):
    m, s = lax.axis_index("mode"), lax.axis_index("space")
    xh, y, c, xl, z_at = m // 8, (m // 2) % 4, m % 2, s // 16, s % 16
    g, yb = y // 2, y % 2
    r = xh * 4 + yb * 2 + c
    slot, q = g * 8 + r, chunk(r)
    r_of = {f: (1 - xh if f[0] else xh) * 4 + (1 - yb if f[1] else yb) * 2 + (1 - c if f[2] else c) for f in FLIPS}
    mode_of = {f: (1 - xh if f[0] else xh) * 8 + (1 - yb if f[1] else yb) * 2 + (1 - c if f[2] else c) for f in FLIPS}
    SELF = FLIPS[7]
    across = (1 - xl) * 16 + z_at
    works, sends = g == 0, g == 1
    low, high = s > 0, s < 31
    first, last = m == 0, m == 1
    get_low, get_high = first & low, last & high
    get_edge = get_low | get_high
    put_kl = (first & high) | (last & low)
    below, above = jnp.maximum(s - 1, 0), jnp.minimum(s + 1, 31)

    loads = [
        pltpu.make_async_copy(a, b, in_sem.at[i])
        for i, (a, b) in enumerate(
            (
                (res_hbm, res.at[:, :, 8:24, :]),
                (part_hbm, part_v),
                (term_hbm, term_v),
                (coef_hbm, coef_v),
                (kl_hbm, klv.at[:, :, 8:24, :]),
                (sol_hbm, sol),
            )
        )
    ]
    for load in loads[:4]:
        load.start()

    barrier = pltpu.get_barrier_semaphore()

    def greet(device):
        pl.semaphore_signal(barrier, inc=1, device_id=device, device_id_type=MESH)

    def along_z(d):
        return m, xl * 16 + (z_at + d) % 16

    @pl.when(get_low)
    def _():
        for t in range(15, -1, -1):
            greet((t, below))

    @pl.when(get_high)
    def _():
        for t in range(15, -1, -1):
            greet((t, above))

    @pl.when(works)
    def _():
        for f in FLIPS:
            greet((mode_of[f] + 4, s))
            greet((mode_of[f] + 4, across))
        for f in FLIPS:
            greet((mode_of[f], across))
            if f != SELF:
                greet((mode_of[f], s))

    greet(along_z(1))
    greet(along_z(15))
    for load in loads[4:]:
        load.start()

    for i in range(2):
        for z in range(2):
            res[i, z, 0:8, :] = jnp.zeros((8, 128), F32)
            res[i, z, 24:32, :] = jnp.zeros((8, 128), F32)
            edges[i, z] = jnp.zeros((8, 128), F32)
    for load in loads[:4]:
        load.wait()
    p = part_v[...]
    ints[0, :, 0:TERMS] = (p % 2) * 16 + (p // 8) % 2 * 8 + p // 16 * 4 + p // 2 % 4
    ints[1, :, 0:TERMS] = term_v[...]
    floats[:, 0:TERMS] = coef_v[...]
    for j in range(8):
        for i in range(2):
            for z in range(2):
                pieces[j, i, 4 * z : 4 * z + 4, :] = res[i, z, 2 * j + 7 : 2 * j + 11, :]
    for i in range(2):
        for z in range(2):
            edges[0, i, 4 * z : 4 * z + 1, :] = res[i, z, 23:24, :]
            edges[1, i, 4 * z + 2 : 4 * z + 3, :] = -res[i, z, 8:9, :]

    pl.semaphore_wait(barrier, 17 + g + low.astype(jnp.int32) + high.astype(jnp.int32))

    def tell(i):
        for d in (1 << i, 16 - (1 << i)):
            pl.semaphore_signal(ring_sem.at[i], inc=1, device_id=along_z(d), device_id_type=MESH)

    def hear(i):
        pl.semaphore_wait(ring_sem.at[i], 2)

    def copy_to(src, dst, send_sem, recv_sem, device):
        return pltpu.make_async_remote_copy(
            src_ref=src, dst_ref=dst, send_sem=send_sem, recv_sem=recv_sem, device_id=device, device_id_type=MESH
        )

    def main_copy(i):
        f = FLIPS[i]
        return copy_to(pieces.at[chunk(r_of[f])], got.at[slot], main_ss, main_rs.at[g * 8 + i], (mode_of[f], s))

    def int_copy(i):
        return copy_to(ints, got_ints.at[slot], int_ss, int_rs.at[g], (mode_of[FLIPS[i]], s))

    def float_copy(i):
        return copy_to(floats, got_floats.at[slot], flo_ss, flo_rs.at[g], (mode_of[FLIPS[i]], s))

    def edge_copy(up):
        to = (0, above) if up else (1, below)
        return copy_to(edges.at[1 - up], got_edges.at[slot], edge_ss.at[up], edge_rs, to)

    def kl_copy():
        return copy_to(kl_edge, got_kl, kle_ss, kle_rs, (m, jnp.where(first, above, below)))

    def all_of(ref, n, send_sem, recv_sem):
        return copy_to(ref.at[pl.ds(0, n)], ref.at[pl.ds(0, n)], send_sem, recv_sem, (m, s))

    @pl.when(high)
    def _():
        edge_copy(1).start()

    @pl.when(low)
    def _():
        edge_copy(0).start()

    for i in range(7):
        int_copy(i).start()
        float_copy(i).start()
    for i in range(7):
        main_copy(i).start()

    @pl.when(sends)
    def _():
        int_copy(7).start()
        float_copy(7).start()
        main_copy(7).start()

    tell(0)

    @pl.when(sends)
    def _():
        for t in (0, 1, 2, 3, 8, 9, 10, 11):
            for to in ((t, s), (t, across)):
                pl.semaphore_signal(here_sem, inc=1, device_id=to, device_id_type=MESH)
        hear(0)
        tell(1)
        hear(1)
        tell(2)

    lane = lax.broadcasted_iota(jnp.int32, (8, 128), 1)
    sub = lax.broadcasted_iota(jnp.int32, (8, 128), 0)
    row = sub % 4
    inner = jnp.where(lane < 127, 0.5, 0.0).astype(F32)
    border = (0.5 + jnp.where(lane == 0, 0.5, 0.0) + jnp.where(lane == 127, 0.5, 0.0)).astype(F32)
    valid = (row == 1) | (row == 2)

    def faces(x, z):
        return jnp.where(sub == 3, pltpu.roll(z, 2, 0), jnp.where(sub == 7, pltpu.roll(z, 5, 0), x))

    def rows(y, own):
        return jnp.where(row == 0, pltpu.roll(own, 7, 0), jnp.where(row == 3, pltpu.roll(own, 1, 0), y))

    def differences(d, tiles):
        for i in range(2):
            v = tiles[i]
            ff[16 * i + d, 0] = faces(v - pltpu.roll(v, 7, 0), v - pltpu.roll(v, 4, 0))
            ff[16 * i + d, 1] = rows(v - pltpu.roll(v, 127, 1), v)

    def take(a, places):
        for i in places:
            copy_to(pieces.at[0], got.at[0], main_ss, main_rs.at[a * 8 + i], (m, s)).wait_recv()
        for i in places:
            d = a * 8 + r_of[FLIPS[i]]
            differences(d, [got[d, 0], got[d, 1]])

    def weigh(h, carry):
        for i in range(2):
            for e in range(TERMS):
                k = int_s[h, 1, i, e]
                w = float_s[h, i, e]
                wa[2 * h + i, e, 0] = w * aa[k, 0]
                wa[2 * h + i, e, 1] = w * aa[k, 1]
        return carry

    def eight_modes(h, carry):
        for j in range(8):
            n = 8 * h + j
            o, i = 4 * h + j // 2, j % 2
            one = aa[0, 0] * ff[16 * i + o, 0]
            two = aa[0, 1] * ff[16 * i + o, 1]
            for e in range(TERMS):
                p = int_s[o, 0, i, e]
                one += wa[n, e, 0] * ff[p, 0]
                two += wa[n, e, 1] * ff[p, 1]
            flux[n, 0] = one
            flux[n, 1] = two
        return carry

    row_0 = jnp.where(row == 0, 1.0, 0.0).astype(F32)
    row_2 = jnp.where(row == 2, 1.0, 0.0).astype(F32)
    last_sub = jnp.where(sub == 7, 1.0, 0.0).astype(F32)

    def finish(n, v, sums):
        norm, curve, energy = sums
        one, two = flux[n, 0], flux[n, 1]
        out = one + two - pltpu.roll(two, 1, 1)
        out += pltpu.roll(row_0 * two - one, 1, 0)
        out += row_2 * pltpu.roll(two - last_sub * one, 7, 0)
        out += jnp.where(sub == 1, pltpu.roll(one, 6, 0), jnp.where(sub == 2, pltpu.roll(one, 3, 0), 0.0))
        out -= jnp.where(sub == 5, pltpu.roll(one, 2, 0), 0.0)
        img[n] = out
        out = jnp.where(valid, out, 0.0)
        v = jnp.where(valid, v, 0.0)
        return norm + v * v, curve + v * out, energy + out * out

    def eight_far_modes(h, sums):
        for j in range(8):
            n = 16 + 8 * h + j
            o, i = 8 + 4 * h + j // 2, j % 2
            one = aa[0, 0] * ff[16 * i + o, 0]
            two = aa[0, 1] * ff[16 * i + o, 1]
            for e in range(TERMS):
                p = int_s[o, 0, i, e]
                k = int_s[o, 1, i, e]
                w = float_s[o, i, e]
                one += w * (aa[k, 0] * ff[p, 0])
                two += w * (aa[k, 1] * ff[p, 1])
            flux[n, 0] = one
            flux[n, 1] = two
            sums = finish(n - 16, got[o - 8, i], sums)
        return sums

    own_sum = xl * 8 + r

    def a_copy(mode, space):
        return copy_to(sum_a, sums_a.at[own_sum], a_ss, a_rs, (mode, space))

    def to_scalars(a):
        half = pl.ds(8 * a, 8)
        copies = [
            pltpu.make_async_copy(got_ints.at[half], int_s.at[half], smem_sem.at[2 * a]),
            pltpu.make_async_copy(got_floats.at[half], float_s.at[half], smem_sem.at[2 * a + 1]),
        ]
        for copy in copies:
            copy.start()
        return copies

    @pl.when(works)
    def _():
        loads[4].wait()
        end = jnp.where(first, 23, 8)
        for z in range(2):
            kl_edge[:, z : z + 1, :] = klv[:, z, pl.ds(end, 1), :]

        @pl.when(put_kl)
        def _():
            kl_copy().start()

        got_ints[slot] = ints[...]
        got_floats[slot] = floats[...]
        hear(0)
        tell(1)

        for z in range(2):
            for r in range(4):
                cof[:, 4 * z + r : 4 * z + r + 1, :] = klv[:, z, pl.ds(2 * q + 7 + r, 1), :]

        @pl.when(first)
        def _():
            cof[:, 0:1, :] = jnp.zeros((KL, 1, 128), F32)
            cof[:, 4:5, :] = jnp.zeros((KL, 1, 128), F32)

        @pl.when(last)
        def _():
            cof[:, 3:4, :] = jnp.zeros((KL, 1, 128), F32)
            cof[:, 7:8, :] = jnp.zeros((KL, 1, 128), F32)

        got[slot] = pieces[q]
        differences(slot, [pieces[q, 0], pieces[q, 1]])

        @pl.when(get_edge)
        def _():
            kl_copy().wait_recv()

        @pl.when(get_low)
        def _():
            cof[:, 0:1, :] = got_kl[:, 0:1, :]
            cof[:, 4:5, :] = got_kl[:, 1:2, :]

        @pl.when(get_high)
        def _():
            cof[:, 3:4, :] = got_kl[:, 0:1, :]
            cof[:, 7:8, :] = got_kl[:, 1:2, :]

        for k in range(KL):
            a = cof[k]
            aa[k, 0] = faces(0.5 * (a + pltpu.roll(a, 7, 0)), 0.5 * (a + pltpu.roll(a, 4, 0)))
            aa[k, 1] = rows(inner * (a + pltpu.roll(a, 127, 1)), border * a)

        hear(1)
        tell(2)
        all_of(got_ints, 7, int_ss, int_rs.at[0]).wait_recv()
        all_of(got_floats, 7, flo_ss, flo_rs.at[0]).wait_recv()
        near = to_scalars(0)
        take(0, range(6, -1, -1))
        for copy in near:
            copy.wait()
        lax.fori_loop(0, 8, weigh, 0)
        all_of(got_ints, 8, int_ss, int_rs.at[1]).wait_recv()
        all_of(got_floats, 8, flo_ss, flo_rs.at[1]).wait_recv()
        far = to_scalars(1)
        take(1, range(7, -1, -1))

        @pl.when(get_edge)
        def _():
            all_of(got_edges, 16, edge_ss.at[0], edge_rs).wait_recv()
            for i in range(2):
                for d in range(16):
                    ff[16 * i + d, 0] = ff[16 * i + d, 0] + got_edges[d, i]

        zero = jnp.zeros((8, 128), F32)
        lax.fori_loop(0, 2, eight_modes, 0)
        for copy in far:
            copy.wait()
        parts = lax.fori_loop(0, 2, eight_far_modes, (zero, zero, zero))
        for n in range(16, MODES):
            parts = finish(n, got[n // 2, n % 2], parts)

        sum_a[...] = jnp.zeros((4, 128), F32)
        for i in range(3):
            sum_a[i : i + 1, :] = jnp.sum(parts[i], axis=0, keepdims=True)
        pl.semaphore_wait(here_sem, 16)
        for other in (0, 4):
            for f in FLIPS:
                a_copy(mode_of[f] + other, across).start()
                if other or f != SELF:
                    a_copy(mode_of[f] + other, s).start()
        sums_a[own_sum] = sum_a[...]
        all_of(sums_a, 15, a_ss, a_rs).wait_recv()

    @pl.when(sends)
    def _():
        all_of(sums_a, 16, a_ss, a_rs).wait_recv()

    def b_copy(d):
        return copy_to(sum_b, sums_b.at[z_at], b_ss, b_rs, along_z(d))

    def back_copy(f, other):
        src = img.at[pl.ds(2 * (r_of[f] + 2 * other), 2)]
        return copy_to(src, back.at[q], back_ss, back_rs, (mode_of[f] + other, s))

    sum_b[...] = jnp.sum(sums_a[...], axis=0)
    hear(2)
    for d in RING:
        b_copy(d).start()
    sums_b[z_at] = sum_b[...]

    @pl.when(works)
    def _():
        for f in FLIPS:
            back_copy(f, 4).start()
            if f != SELF:
                back_copy(f, 0).start()
        back[q] = img[pl.ds(2 * slot, 2)]
        all_of(back, 7, back_ss, back_rs).wait_recv()

    @pl.when(sends)
    def _():
        all_of(back, 8, back_ss, back_rs).wait_recv()

    for i in range(2):
        for z in range(2):
            for h in range(2):
                tile = pltpu.roll(back[4 * h, i], 7 - 4 * z, 0)
                for j in range(1, 4):
                    tile = jnp.where(sub // 2 == j, pltpu.roll(back[4 * h + j, i], (2 * j + 7 - 4 * z) % 8, 0), tile)
                image_ref[i, z, 8 * h : 8 * h + 8, :] = tile
    loads[5].wait()

    @pl.when(works)
    def _():
        all_of(pieces, 7, main_ss, main_rs.at[0]).wait_send()
        all_of(got_ints, 7, int_ss, int_rs.at[0]).wait_send()
        all_of(got_floats, 7, flo_ss, flo_rs.at[0]).wait_send()
        all_of(got, 15, back_ss, back_rs).wait_send()
        all_of(sums_b, 16, a_ss, a_rs).wait_send()
        all_of(sums_b, 15, a_ss, a_rs).wait_send()

    @pl.when(sends)
    def _():
        loads[4].wait()
        all_of(pieces, 8, main_ss, main_rs.at[0]).wait_send()
        all_of(got_ints, 8, int_ss, int_rs.at[0]).wait_send()
        all_of(got_floats, 8, flo_ss, flo_rs.at[0]).wait_send()

    @pl.when(put_kl)
    def _():
        kl_copy().wait_send()

    @pl.when(high)
    def _():
        edge_copy(1).wait_send()

    @pl.when(low)
    def _():
        edge_copy(0).wait_send()

    all_of(sums_b, 15, b_ss, b_rs).wait_recv()
    sums = jnp.sum(jnp.sum(sums_b[...], axis=0), axis=1, keepdims=True)
    norm, curve, energy = sums[0:1], sums[1:2], sums[2:3]
    step = curve / (energy + EPS)
    norm_new = jnp.maximum(norm - 2.0 * step * curve + step * step * energy, 0.0)
    beta = norm_new / (norm + EPS)
    for i in range(2):
        for z in range(2):
            for h in range(2):
                at = pl.ds(8 * h, 8)
                old = res[i, z, 8 + 8 * h : 16 + 8 * h, :]
                sol_ref[i, z, at, :] = sol[i, z, at, :] + step * old
                new = old - step * image_ref[i, z, at, :]
                res_ref[i, z, at, :] = new
                dir_ref[i, z, at, :] = new + beta * old
    all_of(sums_b, 15, b_ss, b_rs).wait_send()


def deliver(*refs):
    sem = refs[8]
    copies = [pltpu.make_async_copy(refs[i], refs[4 + i], sem.at[i]) for i in range(4)]
    for copy in copies:
        copy.start()
    for copy in copies:
        copy.wait()


def on_device(residual, solution, kl_terms, partner, kl_index, coefficient):
    vmem = pl.BlockSpec(memory_space=pltpu.VMEM)
    anywhere = pl.BlockSpec(memory_space=pl.ANY)
    dma = pltpu.SemaphoreType.DMA
    field = pltpu.VMEM(residual.shape, F32)
    i32 = jnp.int32
    results = pl.pallas_call(
        galerkin,
        out_shape=(field,) * 4,
        in_specs=[anywhere] * 6,
        out_specs=(vmem,) * 4,
        scratch_shapes=[
            pltpu.VMEM((2, 2, 32, 128), F32),
            pltpu.VMEM((2, 2, 16, 128), F32),
            pltpu.VMEM((KL, 2, 32, 128), F32),
            pltpu.VMEM((2, TERMS), i32),
            pltpu.VMEM((2, TERMS), i32),
            pltpu.VMEM((2, TERMS), F32),
            pltpu.VMEM((8, 2, 8, 128), F32),
            pltpu.VMEM((2, 2, 8, 128), F32),
            pltpu.VMEM((KL, 2, 128), F32),
            pltpu.VMEM((2, 2, 128), i32),
            pltpu.VMEM((2, 128), F32),
            pltpu.VMEM((16, 2, 8, 128), F32),
            pltpu.VMEM((16, 2, 8, 128), F32),
            pltpu.VMEM((KL, 2, 128), F32),
            pltpu.VMEM((16, 2, 2, 128), i32),
            pltpu.VMEM((16, 2, 128), F32),
            pltpu.SMEM((16, 2, 2, 128), i32),
            pltpu.SMEM((16, 2, 128), F32),
            pltpu.VMEM((KL, 8, 128), F32),
            pltpu.VMEM((KL, 2, 8, 128), F32),
            pltpu.VMEM((MODES // 2, TERMS, 2, 8, 128), F32),
            pltpu.VMEM((MODES, 2, 8, 128), F32),
            pltpu.VMEM((MODES, 2, 8, 128), F32),
            pltpu.VMEM((MODES, 8, 128), F32),
            pltpu.VMEM((8, 2, 8, 128), F32),
            pltpu.VMEM((4, 128), F32),
            pltpu.VMEM((16, 4, 128), F32),
            pltpu.VMEM((4, 128), F32),
            pltpu.VMEM((16, 4, 128), F32),
            dma((6,)),
            dma, dma((16,)),
            dma((2,)), dma,
            dma, dma,
            dma, dma((2,)),
            dma, dma((2,)),
            dma((4,)),
            dma, dma,
            dma, dma,
            dma, dma,
            pltpu.SemaphoreType.REGULAR((3,)),
            pltpu.SemaphoreType.REGULAR,
        ],
        compiler_params=pltpu.CompilerParams(
            collective_id=0, has_side_effects=True, vmem_limit_bytes=60 << 20
        ),
        name="galerkin",
    )(residual, solution, kl_terms, partner, kl_index, coefficient)
    return pl.pallas_call(
        deliver,
        out_shape=(jax.ShapeDtypeStruct(residual.shape, F32),) * 4,
        in_specs=[vmem] * 4,
        out_specs=(anywhere,) * 4,
        scratch_shapes=[dma((4,))],
        compiler_params=pltpu.CompilerParams(vmem_limit_bytes=60 << 20),
        name="deliver",
    )(*(pltpu.with_memory_space_constraint(a, pltpu.VMEM) for a in results))


def solution(mesh):
    field = P("mode", None, "space", None)
    row = P("mode", None)
    return jax.shard_map(
        on_device,
        mesh=mesh,
        in_specs=(field, field, P(None, None, "space", None), row, row, row),
        out_specs=(field, field, field, field),
        check_vma=False,
    )
```

```python
import jax
import jax.numpy as jnp
from jax import lax
from jax.experimental import pallas as pl
from jax.experimental.pallas import tpu as pltpu
from jax.sharding import PartitionSpec as P

EPS = 1e-6
MESH = pl.DeviceIdType.MESH
KL, TERMS, MODES = 21, 24, 32
F32 = jnp.float32


FLIPS = [(a, b, d) for a in (1, 0) for b in ((0, 1) if a else (1, 0)) for d in (1, 0)]
RING = [8, 7, 9, 6, 10, 5, 11, 4, 12, 3, 13, 2, 14, 1, 15]


def chunk(r):
    return jnp.where(r == 0, 0, jnp.where(r == 1, 7, r - 1))


def galerkin(
    res_hbm, sol_hbm, kl_hbm, part_hbm, term_hbm, coef_hbm,
    image_ref, sol_ref, res_ref, dir_ref,
    res, sol, klv, part_v, term_v, coef_v,
    pieces, edges, kl_edge, ints, floats,
    got, got_edges, got_kl, got_ints, got_floats, int_s, float_s,
    cof, aa, wa, ff, flux, img, back, sum_a, sums_a, sum_b, sums_b,
    in_sem, main_ss, main_rs, edge_ss, edge_rs, kle_ss, kle_rs,
    int_ss, int_rs, flo_ss, flo_rs, smem_sem,
    a_ss, a_rs, b_ss, b_rs, back_ss, back_rs, ring_sem, here_sem,
):
    m, s = lax.axis_index("mode"), lax.axis_index("space")
    xh, y, c, xl, z_at = m // 8, (m // 2) % 4, m % 2, s // 16, s % 16
    g, yb = y // 2, y % 2
    r = xh * 4 + yb * 2 + c
    slot, q = g * 8 + r, chunk(r)
    r_of = {f: (1 - xh if f[0] else xh) * 4 + (1 - yb if f[1] else yb) * 2 + (1 - c if f[2] else c) for f in FLIPS}
    mode_of = {f: (1 - xh if f[0] else xh) * 8 + (1 - yb if f[1] else yb) * 2 + (1 - c if f[2] else c) for f in FLIPS}
    SELF = FLIPS[7]
    across = (1 - xl) * 16 + z_at
    works, sends = g == 0, g == 1
    low, high = s > 0, s < 31
    first, last = m == 0, m == 1
    get_low, get_high = first & low, last & high
    get_edge = get_low | get_high
    put_kl = (first & high) | (last & low)
    below, above = jnp.maximum(s - 1, 0), jnp.minimum(s + 1, 31)

    loads = [
        pltpu.make_async_copy(a, b, in_sem.at[i])
        for i, (a, b) in enumerate(
            (
                (res_hbm, res.at[:, :, 8:24, :]),
                (part_hbm, part_v),
                (term_hbm, term_v),
                (coef_hbm, coef_v),
                (kl_hbm, klv.at[:, :, 8:24, :]),
                (sol_hbm, sol),
            )
        )
    ]
    for load in loads[:4]:
        load.start()

    barrier = pltpu.get_barrier_semaphore()

    def greet(device):
        pl.semaphore_signal(barrier, inc=1, device_id=device, device_id_type=MESH)

    def along_z(d):
        return m, xl * 16 + (z_at + d) % 16

    @pl.when(get_low)
    def _():
        for t in range(15, -1, -1):
            greet((t, below))

    @pl.when(get_high)
    def _():
        for t in range(15, -1, -1):
            greet((t, above))

    @pl.when(works)
    def _():
        for f in FLIPS:
            greet((mode_of[f] + 4, s))
            greet((mode_of[f] + 4, across))
        for f in FLIPS:
            greet((mode_of[f], across))
            if f != SELF:
                greet((mode_of[f], s))

    greet(along_z(1))
    greet(along_z(15))
    for load in loads[4:]:
        load.start()

    for i in range(2):
        for z in range(2):
            res[i, z, 0:8, :] = jnp.zeros((8, 128), F32)
            res[i, z, 24:32, :] = jnp.zeros((8, 128), F32)
            edges[i, z] = jnp.zeros((8, 128), F32)
    for load in loads[:4]:
        load.wait()
    p = part_v[...]
    p = (p % 2) * 16 + (p // 8) % 2 * 8 + p // 16 * 4 + p // 2 % 4
    for i in range(2):
        ints[:, TERMS * i : TERMS * (i + 1)] = p[i : i + 1, :]
        ints[:, TERMS * (i + 2) : TERMS * (i + 3)] = term_v[i : i + 1, :]
        floats[:, TERMS * i : TERMS * (i + 1)] = coef_v[i : i + 1, :]
    for j in range(8):
        for i in range(2):
            for z in range(2):
                pieces[j, i, 4 * z : 4 * z + 4, :] = res[i, z, 2 * j + 7 : 2 * j + 11, :]
    for i in range(2):
        for z in range(2):
            edges[0, i, 4 * z : 4 * z + 1, :] = res[i, z, 23:24, :]
            edges[1, i, 4 * z + 2 : 4 * z + 3, :] = -res[i, z, 8:9, :]

    pl.semaphore_wait(barrier, 17 + g + low.astype(jnp.int32) + high.astype(jnp.int32))

    def tell(i):
        for d in (1 << i, 16 - (1 << i)):
            pl.semaphore_signal(ring_sem.at[i], inc=1, device_id=along_z(d), device_id_type=MESH)

    def hear(i):
        pl.semaphore_wait(ring_sem.at[i], 2)

    def copy_to(src, dst, send_sem, recv_sem, device):
        return pltpu.make_async_remote_copy(
            src_ref=src, dst_ref=dst, send_sem=send_sem, recv_sem=recv_sem, device_id=device, device_id_type=MESH
        )

    def main_copy(i):
        f = FLIPS[i]
        return copy_to(pieces.at[chunk(r_of[f])], got.at[slot], main_ss, main_rs.at[g * 8 + i], (mode_of[f], s))

    def int_copy(i):
        return copy_to(ints, got_ints.at[slot], int_ss, int_rs.at[g], (mode_of[FLIPS[i]], s))

    def float_copy(i):
        return copy_to(floats, got_floats.at[slot], flo_ss, flo_rs.at[g], (mode_of[FLIPS[i]], s))

    def edge_copy(up):
        to = (0, above) if up else (1, below)
        return copy_to(edges.at[1 - up], got_edges.at[slot], edge_ss.at[up], edge_rs, to)

    def kl_copy():
        return copy_to(kl_edge, got_kl, kle_ss, kle_rs, (m, jnp.where(first, above, below)))

    def all_of(ref, n, send_sem, recv_sem):
        return copy_to(ref.at[pl.ds(0, n)], ref.at[pl.ds(0, n)], send_sem, recv_sem, (m, s))

    @pl.when(high)
    def _():
        edge_copy(1).start()

    @pl.when(low)
    def _():
        edge_copy(0).start()

    for i in range(7):
        int_copy(i).start()
        float_copy(i).start()
    for i in range(7):
        main_copy(i).start()

    @pl.when(sends)
    def _():
        int_copy(7).start()
        float_copy(7).start()
        main_copy(7).start()

    tell(0)

    @pl.when(sends)
    def _():
        for t in (0, 1, 2, 3, 8, 9, 10, 11):
            for to in ((t, s), (t, across)):
                pl.semaphore_signal(here_sem, inc=1, device_id=to, device_id_type=MESH)
        hear(0)
        tell(1)
        hear(1)
        tell(2)

    lane = lax.broadcasted_iota(jnp.int32, (8, 128), 1)
    sub = lax.broadcasted_iota(jnp.int32, (8, 128), 0)
    row = sub % 4
    inner = jnp.where(lane < 127, 0.5, 0.0).astype(F32)
    border = (0.5 + jnp.where(lane == 0, 0.5, 0.0) + jnp.where(lane == 127, 0.5, 0.0)).astype(F32)
    valid = (row == 1) | (row == 2)

    def faces(x, z):
        return jnp.where(sub == 3, pltpu.roll(z, 2, 0), jnp.where(sub == 7, pltpu.roll(z, 5, 0), x))

    def rows(y, own):
        return jnp.where(row == 0, pltpu.roll(own, 7, 0), jnp.where(row == 3, pltpu.roll(own, 1, 0), y))

    def differences(d, tiles):
        for i in range(2):
            v = tiles[i]
            ff[16 * i + d, 0] = faces(v - pltpu.roll(v, 7, 0), v - pltpu.roll(v, 4, 0))
            ff[16 * i + d, 1] = rows(v - pltpu.roll(v, 127, 1), v)

    def take(a, places):
        for i in places:
            copy_to(pieces.at[0], got.at[0], main_ss, main_rs.at[a * 8 + i], (m, s)).wait_recv()
        for i in places:
            d = a * 8 + r_of[FLIPS[i]]
            differences(d, [got[d, 0], got[d, 1]])

    def weigh(h, carry):
        for i in range(2):
            for e in range(TERMS):
                k = int_s[h, 0, TERMS * (i + 2) + e]
                w = float_s[h, 0, TERMS * i + e]
                wa[2 * h + i, e, 0] = w * aa[k, 0]
                wa[2 * h + i, e, 1] = w * aa[k, 1]
        return carry

    def eight_modes(h, carry):
        for j in range(8):
            n = 8 * h + j
            o, i = 4 * h + j // 2, j % 2
            one = aa[0, 0] * ff[16 * i + o, 0]
            two = aa[0, 1] * ff[16 * i + o, 1]
            for e in range(TERMS):
                p = int_s[o, 0, TERMS * i + e]
                one += wa[n, e, 0] * ff[p, 0]
                two += wa[n, e, 1] * ff[p, 1]
            flux[n, 0] = one
            flux[n, 1] = two
        return carry

    row_0 = jnp.where(row == 0, 1.0, 0.0).astype(F32)
    row_2 = jnp.where(row == 2, 1.0, 0.0).astype(F32)
    last_sub = jnp.where(sub == 7, 1.0, 0.0).astype(F32)

    def finish(n, v, sums):
        norm, curve, energy = sums
        one, two = flux[n, 0], flux[n, 1]
        out = one + two - pltpu.roll(two, 1, 1)
        out += pltpu.roll(row_0 * two - one, 1, 0)
        out += row_2 * pltpu.roll(two - last_sub * one, 7, 0)
        out += jnp.where(sub == 1, pltpu.roll(one, 6, 0), jnp.where(sub == 2, pltpu.roll(one, 3, 0), 0.0))
        out -= jnp.where(sub == 5, pltpu.roll(one, 2, 0), 0.0)
        img[n] = out
        out = jnp.where(valid, out, 0.0)
        v = jnp.where(valid, v, 0.0)
        return norm + v * v, curve + v * out, energy + out * out

    def eight_far_modes(h, sums):
        for j in range(8):
            n = 16 + 8 * h + j
            o, i = 8 + 4 * h + j // 2, j % 2
            one = aa[0, 0] * ff[16 * i + o, 0]
            two = aa[0, 1] * ff[16 * i + o, 1]
            for e in range(TERMS):
                p = int_s[o, 0, TERMS * i + e]
                k = int_s[o, 0, TERMS * (i + 2) + e]
                w = float_s[o, 0, TERMS * i + e]
                one += w * (aa[k, 0] * ff[p, 0])
                two += w * (aa[k, 1] * ff[p, 1])
            flux[n, 0] = one
            flux[n, 1] = two
            sums = finish(n - 16, got[o - 8, i], sums)
        return sums

    own_sum = xl * 8 + r

    def a_copy(mode, space):
        return copy_to(sum_a, sums_a.at[own_sum], a_ss, a_rs, (mode, space))

    def to_scalars(a):
        half = pl.ds(8 * a, 8)
        copies = [
            pltpu.make_async_copy(got_ints.at[half], int_s.at[half], smem_sem.at[2 * a]),
            pltpu.make_async_copy(got_floats.at[half], float_s.at[half], smem_sem.at[2 * a + 1]),
        ]
        for copy in copies:
            copy.start()
        return copies

    @pl.when(works)
    def _():
        loads[4].wait()
        end = jnp.where(first, 23, 8)
        for z in range(2):
            kl_edge[:, z : z + 1, :] = klv[:, z, pl.ds(end, 1), :]

        @pl.when(put_kl)
        def _():
            kl_copy().start()

        got_ints[slot] = ints[...]
        got_floats[slot] = floats[...]
        hear(0)
        tell(1)

        for z in range(2):
            for r in range(4):
                cof[:, 4 * z + r : 4 * z + r + 1, :] = klv[:, z, pl.ds(2 * q + 7 + r, 1), :]

        @pl.when(first)
        def _():
            cof[:, 0:1, :] = jnp.zeros((KL, 1, 128), F32)
            cof[:, 4:5, :] = jnp.zeros((KL, 1, 128), F32)

        @pl.when(last)
        def _():
            cof[:, 3:4, :] = jnp.zeros((KL, 1, 128), F32)
            cof[:, 7:8, :] = jnp.zeros((KL, 1, 128), F32)

        got[slot] = pieces[q]
        differences(slot, [pieces[q, 0], pieces[q, 1]])

        @pl.when(get_edge)
        def _():
            kl_copy().wait_recv()

        @pl.when(get_low)
        def _():
            cof[:, 0:1, :] = got_kl[:, 0:1, :]
            cof[:, 4:5, :] = got_kl[:, 1:2, :]

        @pl.when(get_high)
        def _():
            cof[:, 3:4, :] = got_kl[:, 0:1, :]
            cof[:, 7:8, :] = got_kl[:, 1:2, :]

        for k in range(KL):
            a = cof[k]
            aa[k, 0] = faces(0.5 * (a + pltpu.roll(a, 7, 0)), 0.5 * (a + pltpu.roll(a, 4, 0)))
            aa[k, 1] = rows(inner * (a + pltpu.roll(a, 127, 1)), border * a)

        hear(1)
        tell(2)
        all_of(got_ints, 7, int_ss, int_rs.at[0]).wait_recv()
        all_of(got_floats, 7, flo_ss, flo_rs.at[0]).wait_recv()
        near = to_scalars(0)
        take(0, range(6, -1, -1))
        for copy in near:
            copy.wait()
        lax.fori_loop(0, 8, weigh, 0)
        all_of(got_ints, 8, int_ss, int_rs.at[1]).wait_recv()
        all_of(got_floats, 8, flo_ss, flo_rs.at[1]).wait_recv()
        far = to_scalars(1)
        take(1, range(7, -1, -1))

        @pl.when(get_edge)
        def _():
            all_of(got_edges, 16, edge_ss.at[0], edge_rs).wait_recv()
            for i in range(2):
                for d in range(16):
                    ff[16 * i + d, 0] = ff[16 * i + d, 0] + got_edges[d, i]

        zero = jnp.zeros((8, 128), F32)
        lax.fori_loop(0, 2, eight_modes, 0)
        for copy in far:
            copy.wait()
        parts = lax.fori_loop(0, 2, eight_far_modes, (zero, zero, zero))
        for n in range(16, MODES):
            parts = finish(n, got[n // 2, n % 2], parts)

        sum_a[...] = jnp.zeros((4, 128), F32)
        for i in range(3):
            sum_a[i : i + 1, :] = jnp.sum(parts[i], axis=0, keepdims=True)
        pl.semaphore_wait(here_sem, 16)
        for other in (0, 4):
            for f in FLIPS:
                a_copy(mode_of[f] + other, across).start()
                if other or f != SELF:
                    a_copy(mode_of[f] + other, s).start()
        sums_a[own_sum] = sum_a[...]
        all_of(sums_a, 15, a_ss, a_rs).wait_recv()

    @pl.when(sends)
    def _():
        all_of(sums_a, 16, a_ss, a_rs).wait_recv()

    def b_copy(d):
        return copy_to(sum_b, sums_b.at[z_at], b_ss, b_rs, along_z(d))

    def back_copy(f, other):
        src = img.at[pl.ds(2 * (r_of[f] + 2 * other), 2)]
        return copy_to(src, back.at[q], back_ss, back_rs, (mode_of[f] + other, s))

    sum_b[...] = jnp.sum(sums_a[...], axis=0)
    hear(2)
    for d in RING:
        b_copy(d).start()
    sums_b[z_at] = sum_b[...]

    @pl.when(works)
    def _():
        for f in FLIPS:
            back_copy(f, 4).start()
            if f != SELF:
                back_copy(f, 0).start()
        back[q] = img[pl.ds(2 * slot, 2)]
        all_of(back, 7, back_ss, back_rs).wait_recv()

    @pl.when(sends)
    def _():
        all_of(back, 8, back_ss, back_rs).wait_recv()

    for i in range(2):
        for z in range(2):
            for h in range(2):
                tile = pltpu.roll(back[4 * h, i], 7 - 4 * z, 0)
                for j in range(1, 4):
                    tile = jnp.where(sub // 2 == j, pltpu.roll(back[4 * h + j, i], (2 * j + 7 - 4 * z) % 8, 0), tile)
                image_ref[i, z, 8 * h : 8 * h + 8, :] = tile
    loads[5].wait()

    @pl.when(works)
    def _():
        all_of(pieces, 7, main_ss, main_rs.at[0]).wait_send()
        all_of(got_ints, 7, int_ss, int_rs.at[0]).wait_send()
        all_of(got_floats, 7, flo_ss, flo_rs.at[0]).wait_send()
        all_of(got, 15, back_ss, back_rs).wait_send()
        all_of(sums_b, 16, a_ss, a_rs).wait_send()
        all_of(sums_b, 15, a_ss, a_rs).wait_send()

    @pl.when(sends)
    def _():
        loads[4].wait()
        all_of(pieces, 8, main_ss, main_rs.at[0]).wait_send()
        all_of(got_ints, 8, int_ss, int_rs.at[0]).wait_send()
        all_of(got_floats, 8, flo_ss, flo_rs.at[0]).wait_send()

    @pl.when(put_kl)
    def _():
        kl_copy().wait_send()

    @pl.when(high)
    def _():
        edge_copy(1).wait_send()

    @pl.when(low)
    def _():
        edge_copy(0).wait_send()

    all_of(sums_b, 15, b_ss, b_rs).wait_recv()
    sums = jnp.sum(jnp.sum(sums_b[...], axis=0), axis=1, keepdims=True)
    norm, curve, energy = sums[0:1], sums[1:2], sums[2:3]
    step = curve / (energy + EPS)
    norm_new = jnp.maximum(norm - 2.0 * step * curve + step * step * energy, 0.0)
    beta = norm_new / (norm + EPS)
    for i in range(2):
        for z in range(2):
            for h in range(2):
                at = pl.ds(8 * h, 8)
                old = res[i, z, 8 + 8 * h : 16 + 8 * h, :]
                sol_ref[i, z, at, :] = sol[i, z, at, :] + step * old
                new = old - step * image_ref[i, z, at, :]
                res_ref[i, z, at, :] = new
                dir_ref[i, z, at, :] = new + beta * old
    all_of(sums_b, 15, b_ss, b_rs).wait_send()


def deliver(*refs):
    sem = refs[8]
    copies = [pltpu.make_async_copy(refs[i], refs[4 + i], sem.at[i]) for i in range(4)]
    for copy in copies:
        copy.start()
    for copy in copies:
        copy.wait()


def on_device(residual, solution, kl_terms, partner, kl_index, coefficient):
    vmem = pl.BlockSpec(memory_space=pltpu.VMEM)
    anywhere = pl.BlockSpec(memory_space=pl.ANY)
    dma = pltpu.SemaphoreType.DMA
    field = pltpu.VMEM(residual.shape, F32)
    i32 = jnp.int32
    results = pl.pallas_call(
        galerkin,
        out_shape=(field,) * 4,
        in_specs=[anywhere] * 6,
        out_specs=(vmem,) * 4,
        scratch_shapes=[
            pltpu.VMEM((2, 2, 32, 128), F32),
            pltpu.VMEM((2, 2, 16, 128), F32),
            pltpu.VMEM((KL, 2, 32, 128), F32),
            pltpu.VMEM((2, TERMS), i32),
            pltpu.VMEM((2, TERMS), i32),
            pltpu.VMEM((2, TERMS), F32),
            pltpu.VMEM((8, 2, 8, 128), F32),
            pltpu.VMEM((2, 2, 8, 128), F32),
            pltpu.VMEM((KL, 2, 128), F32),
            pltpu.VMEM((1, 128), i32),
            pltpu.VMEM((1, 128), F32),
            pltpu.VMEM((16, 2, 8, 128), F32),
            pltpu.VMEM((16, 2, 8, 128), F32),
            pltpu.VMEM((KL, 2, 128), F32),
            pltpu.VMEM((16, 1, 128), i32),
            pltpu.VMEM((16, 1, 128), F32),
            pltpu.SMEM((16, 1, 128), i32),
            pltpu.SMEM((16, 1, 128), F32),
            pltpu.VMEM((KL, 8, 128), F32),
            pltpu.VMEM((KL, 2, 8, 128), F32),
            pltpu.VMEM((MODES // 2, TERMS, 2, 8, 128), F32),
            pltpu.VMEM((MODES, 2, 8, 128), F32),
            pltpu.VMEM((MODES, 2, 8, 128), F32),
            pltpu.VMEM((MODES, 8, 128), F32),
            pltpu.VMEM((8, 2, 8, 128), F32),
            pltpu.VMEM((4, 128), F32),
            pltpu.VMEM((16, 4, 128), F32),
            pltpu.VMEM((4, 128), F32),
            pltpu.VMEM((16, 4, 128), F32),
            dma((6,)),
            dma, dma((16,)),
            dma((2,)), dma,
            dma, dma,
            dma, dma((2,)),
            dma, dma((2,)),
            dma((4,)),
            dma, dma,
            dma, dma,
            dma, dma,
            pltpu.SemaphoreType.REGULAR((3,)),
            pltpu.SemaphoreType.REGULAR,
        ],
        compiler_params=pltpu.CompilerParams(
            collective_id=0, has_side_effects=True, vmem_limit_bytes=60 << 20
        ),
        name="galerkin",
    )(residual, solution, kl_terms, partner, kl_index, coefficient)
    return pl.pallas_call(
        deliver,
        out_shape=(jax.ShapeDtypeStruct(residual.shape, F32),) * 4,
        in_specs=[vmem] * 4,
        out_specs=(anywhere,) * 4,
        scratch_shapes=[dma((4,))],
        compiler_params=pltpu.CompilerParams(vmem_limit_bytes=60 << 20),
        name="deliver",
    )(*(pltpu.with_memory_space_constraint(a, pltpu.VMEM) for a in results))


def solution(mesh):
    field = P("mode", None, "space", None)
    row = P("mode", None)
    return jax.shard_map(
        on_device,
        mesh=mesh,
        in_specs=(field, field, P(None, None, "space", None), row, row, row),
        out_specs=(field, field, field, field),
        check_vma=False,
    )
```

```python
import jax
import jax.numpy as jnp
from jax import lax
from jax.experimental import pallas as pl
from jax.experimental.pallas import tpu as pltpu
from jax.sharding import PartitionSpec as P

EPS = 1e-6
MESH = pl.DeviceIdType.MESH
KL, TERMS, MODES = 21, 24, 32
F32 = jnp.float32


FLIPS = [(a, b, d) for a in (1, 0) for b in ((0, 1) if a else (1, 0)) for d in (1, 0)]
RING = [8, 7, 9, 6, 10, 5, 11, 4, 12, 3, 13, 2, 14, 1, 15]


def chunk(r):
    return jnp.where(r == 0, 0, jnp.where(r == 1, 7, r - 1))


def galerkin(
    res_hbm, sol_hbm, kl_hbm, part_hbm, term_hbm, coef_hbm,
    image_ref, sol_ref, res_ref, dir_ref,
    res, sol, klv, part_v, term_v, coef_v,
    pieces, edges, kl_edge, ints, floats,
    got, got_edges, got_kl, got_ints, got_floats, int_s, float_s,
    cof, aa, wa, ff, flux, img, back, sum_a, sums_a, sum_b, sums_b,
    in_sem, main_ss, main_rs, edge_ss, edge_rs, kle_ss, kle_rs,
    int_ss, int_rs, flo_ss, flo_rs, smem_sem,
    a_ss, a_rs, b_ss, b_rs, back_ss, back_rs, ring_sem, here_sem,
):
    m, s = lax.axis_index("mode"), lax.axis_index("space")
    xh, y, c, xl, z_at = m // 8, (m // 2) % 4, m % 2, s // 16, s % 16
    g, yb = y // 2, y % 2
    r = xh * 4 + yb * 2 + c
    slot, q = g * 8 + r, chunk(r)
    r_of = {f: (1 - xh if f[0] else xh) * 4 + (1 - yb if f[1] else yb) * 2 + (1 - c if f[2] else c) for f in FLIPS}
    mode_of = {f: (1 - xh if f[0] else xh) * 8 + (1 - yb if f[1] else yb) * 2 + (1 - c if f[2] else c) for f in FLIPS}
    SELF = FLIPS[7]
    across = (1 - xl) * 16 + z_at
    works, sends = g == 0, g == 1
    low, high = s > 0, s < 31
    first, last = m == 0, m == 1
    get_low, get_high = first & low, last & high
    get_edge = get_low | get_high
    put_kl = (first & high) | (last & low)
    below, above = jnp.maximum(s - 1, 0), jnp.minimum(s + 1, 31)

    loads = [
        pltpu.make_async_copy(a, b, in_sem.at[i])
        for i, (a, b) in enumerate(
            (
                (res_hbm, res.at[:, :, 8:24, :]),
                (part_hbm, part_v),
                (term_hbm, term_v),
                (coef_hbm, coef_v),
                (kl_hbm, klv.at[:, :, 8:24, :]),
                (sol_hbm, sol),
            )
        )
    ]
    for load in loads[:4]:
        load.start()

    barrier = pltpu.get_barrier_semaphore()

    def greet(device):
        pl.semaphore_signal(barrier, inc=1, device_id=device, device_id_type=MESH)

    def along_z(d):
        return m, xl * 16 + (z_at + d) % 16

    @pl.when(get_low)
    def _():
        for t in range(15, -1, -1):
            greet((t, below))

    @pl.when(get_high)
    def _():
        for t in range(15, -1, -1):
            greet((t, above))

    @pl.when(works)
    def _():
        for f in FLIPS:
            greet((mode_of[f] + 4, s))
            greet((mode_of[f] + 4, across))
        for f in FLIPS:
            greet((mode_of[f], across))
            if f != SELF:
                greet((mode_of[f], s))

    greet(along_z(1))
    greet(along_z(15))
    for load in loads[4:]:
        load.start()

    for i in range(2):
        for z in range(2):
            res[i, z, 0:8, :] = jnp.zeros((8, 128), F32)
            res[i, z, 24:32, :] = jnp.zeros((8, 128), F32)
            edges[i, z] = jnp.zeros((8, 128), F32)
    for load in loads[:4]:
        load.wait()
    p = part_v[...]
    p = (p % 2) * 16 + (p // 8) % 2 * 8 + p // 16 * 4 + p // 2 % 4
    for i in range(2):
        ints[:, TERMS * i : TERMS * (i + 1)] = p[i : i + 1, :]
        ints[:, TERMS * (i + 2) : TERMS * (i + 3)] = term_v[i : i + 1, :]
        floats[:, TERMS * i : TERMS * (i + 1)] = coef_v[i : i + 1, :]
    for j in range(8):
        for i in range(2):
            for z in range(2):
                pieces[j, i, 4 * z : 4 * z + 4, :] = res[i, z, 2 * j + 7 : 2 * j + 11, :]
    for i in range(2):
        for z in range(2):
            edges[0, i, 4 * z : 4 * z + 1, :] = res[i, z, 23:24, :]
            edges[1, i, 4 * z + 2 : 4 * z + 3, :] = -res[i, z, 8:9, :]

    pl.semaphore_wait(barrier, 17 + g + low.astype(jnp.int32) + high.astype(jnp.int32))

    def tell(i):
        for d in (1 << i, 16 - (1 << i)):
            pl.semaphore_signal(ring_sem.at[i], inc=1, device_id=along_z(d), device_id_type=MESH)

    def hear(i):
        pl.semaphore_wait(ring_sem.at[i], 2)

    def copy_to(src, dst, send_sem, recv_sem, device):
        return pltpu.make_async_remote_copy(
            src_ref=src, dst_ref=dst, send_sem=send_sem, recv_sem=recv_sem, device_id=device, device_id_type=MESH
        )

    def main_copy(i):
        f = FLIPS[i]
        return copy_to(pieces.at[chunk(r_of[f])], got.at[slot], main_ss, main_rs.at[g * 8 + i], (mode_of[f], s))

    def int_copy(i):
        return copy_to(ints, got_ints.at[slot], int_ss, int_rs.at[g], (mode_of[FLIPS[i]], s))

    def float_copy(i):
        return copy_to(floats, got_floats.at[slot], flo_ss, flo_rs.at[g], (mode_of[FLIPS[i]], s))

    def edge_copy(up):
        to = (0, above) if up else (1, below)
        return copy_to(edges.at[1 - up], got_edges.at[slot], edge_ss.at[up], edge_rs, to)

    def kl_copy():
        return copy_to(kl_edge, got_kl, kle_ss, kle_rs, (m, jnp.where(first, above, below)))

    def all_of(ref, n, send_sem, recv_sem):
        return copy_to(ref.at[pl.ds(0, n)], ref.at[pl.ds(0, n)], send_sem, recv_sem, (m, s))

    @pl.when(high)
    def _():
        edge_copy(1).start()

    @pl.when(low)
    def _():
        edge_copy(0).start()

    for i in range(7):
        int_copy(i).start()
        float_copy(i).start()

    @pl.when(sends)
    def _():
        int_copy(7).start()
        float_copy(7).start()

    for i in range(7):
        main_copy(i).start()

    @pl.when(sends)
    def _():
        main_copy(7).start()

    tell(0)

    @pl.when(sends)
    def _():
        for t in (0, 1, 2, 3, 8, 9, 10, 11):
            for to in ((t, s), (t, across)):
                pl.semaphore_signal(here_sem, inc=1, device_id=to, device_id_type=MESH)
        hear(0)
        tell(1)
        hear(1)
        tell(2)

    lane = lax.broadcasted_iota(jnp.int32, (8, 128), 1)
    sub = lax.broadcasted_iota(jnp.int32, (8, 128), 0)
    row = sub % 4
    inner = jnp.where(lane < 127, 0.5, 0.0).astype(F32)
    border = (0.5 + jnp.where(lane == 0, 0.5, 0.0) + jnp.where(lane == 127, 0.5, 0.0)).astype(F32)
    valid = (row == 1) | (row == 2)

    def faces(x, z):
        return jnp.where(sub == 3, pltpu.roll(z, 2, 0), jnp.where(sub == 7, pltpu.roll(z, 5, 0), x))

    def rows(y, own):
        return jnp.where(row == 0, pltpu.roll(own, 7, 0), jnp.where(row == 3, pltpu.roll(own, 1, 0), y))

    def differences(d, tiles):
        for i in range(2):
            v = tiles[i]
            ff[16 * i + d, 0] = faces(v - pltpu.roll(v, 7, 0), v - pltpu.roll(v, 4, 0))
            ff[16 * i + d, 1] = rows(v - pltpu.roll(v, 127, 1), v)

    def take(a, places):
        for i in places:
            copy_to(pieces.at[0], got.at[0], main_ss, main_rs.at[a * 8 + i], (m, s)).wait_recv()
        for i in places:
            d = a * 8 + r_of[FLIPS[i]]
            differences(d, [got[d, 0], got[d, 1]])

    def weigh(h, carry):
        for i in range(2):
            for e in range(TERMS):
                k = int_s[h, 0, TERMS * (i + 2) + e]
                w = float_s[h, 0, TERMS * i + e]
                wa[2 * h + i, e, 0] = w * aa[k, 0]
                wa[2 * h + i, e, 1] = w * aa[k, 1]
        return carry

    def eight_modes(h, carry):
        for j in range(8):
            n = 8 * h + j
            o, i = 4 * h + j // 2, j % 2
            one = aa[0, 0] * ff[16 * i + o, 0]
            two = aa[0, 1] * ff[16 * i + o, 1]
            for e in range(TERMS):
                p = int_s[o, 0, TERMS * i + e]
                one += wa[n, e, 0] * ff[p, 0]
                two += wa[n, e, 1] * ff[p, 1]
            flux[n, 0] = one
            flux[n, 1] = two
        return carry

    row_0 = jnp.where(row == 0, 1.0, 0.0).astype(F32)
    row_2 = jnp.where(row == 2, 1.0, 0.0).astype(F32)
    last_sub = jnp.where(sub == 7, 1.0, 0.0).astype(F32)

    def finish(n, v, sums):
        norm, curve, energy = sums
        one, two = flux[n, 0], flux[n, 1]
        out = one + two - pltpu.roll(two, 1, 1)
        out += pltpu.roll(row_0 * two - one, 1, 0)
        out += row_2 * pltpu.roll(two - last_sub * one, 7, 0)
        out += jnp.where(sub == 1, pltpu.roll(one, 6, 0), jnp.where(sub == 2, pltpu.roll(one, 3, 0), 0.0))
        out -= jnp.where(sub == 5, pltpu.roll(one, 2, 0), 0.0)
        img[n] = out
        out = jnp.where(valid, out, 0.0)
        v = jnp.where(valid, v, 0.0)
        return norm + v * v, curve + v * out, energy + out * out

    def eight_far_modes(h, sums):
        for j in range(8):
            n = 16 + 8 * h + j
            o, i = 8 + 4 * h + j // 2, j % 2
            one = aa[0, 0] * ff[16 * i + o, 0]
            two = aa[0, 1] * ff[16 * i + o, 1]
            for e in range(TERMS):
                p = int_s[o, 0, TERMS * i + e]
                k = int_s[o, 0, TERMS * (i + 2) + e]
                w = float_s[o, 0, TERMS * i + e]
                one += w * (aa[k, 0] * ff[p, 0])
                two += w * (aa[k, 1] * ff[p, 1])
            flux[n, 0] = one
            flux[n, 1] = two
            sums = finish(n - 16, got[o - 8, i], sums)
        return sums

    own_sum = xl * 8 + r

    def a_copy(mode, space):
        return copy_to(sum_a, sums_a.at[own_sum], a_ss, a_rs, (mode, space))

    def to_scalars(a):
        half = pl.ds(8 * a, 8)
        copies = [
            pltpu.make_async_copy(got_ints.at[half], int_s.at[half], smem_sem.at[2 * a]),
            pltpu.make_async_copy(got_floats.at[half], float_s.at[half], smem_sem.at[2 * a + 1]),
        ]
        for copy in copies:
            copy.start()
        return copies

    @pl.when(works)
    def _():
        loads[4].wait()
        end = jnp.where(first, 23, 8)
        for z in range(2):
            kl_edge[:, z : z + 1, :] = klv[:, z, pl.ds(end, 1), :]

        @pl.when(put_kl)
        def _():
            kl_copy().start()

        got_ints[slot] = ints[...]
        got_floats[slot] = floats[...]
        hear(0)
        tell(1)

        for z in range(2):
            for r in range(4):
                cof[:, 4 * z + r : 4 * z + r + 1, :] = klv[:, z, pl.ds(2 * q + 7 + r, 1), :]

        @pl.when(first)
        def _():
            cof[:, 0:1, :] = jnp.zeros((KL, 1, 128), F32)
            cof[:, 4:5, :] = jnp.zeros((KL, 1, 128), F32)

        @pl.when(last)
        def _():
            cof[:, 3:4, :] = jnp.zeros((KL, 1, 128), F32)
            cof[:, 7:8, :] = jnp.zeros((KL, 1, 128), F32)

        got[slot] = pieces[q]
        differences(slot, [pieces[q, 0], pieces[q, 1]])

        @pl.when(get_edge)
        def _():
            kl_copy().wait_recv()

        @pl.when(get_low)
        def _():
            cof[:, 0:1, :] = got_kl[:, 0:1, :]
            cof[:, 4:5, :] = got_kl[:, 1:2, :]

        @pl.when(get_high)
        def _():
            cof[:, 3:4, :] = got_kl[:, 0:1, :]
            cof[:, 7:8, :] = got_kl[:, 1:2, :]

        for k in range(KL):
            a = cof[k]
            aa[k, 0] = faces(0.5 * (a + pltpu.roll(a, 7, 0)), 0.5 * (a + pltpu.roll(a, 4, 0)))
            aa[k, 1] = rows(inner * (a + pltpu.roll(a, 127, 1)), border * a)

        hear(1)
        tell(2)
        all_of(got_ints, 7, int_ss, int_rs.at[0]).wait_recv()
        all_of(got_floats, 7, flo_ss, flo_rs.at[0]).wait_recv()
        near = to_scalars(0)
        take(0, range(6, -1, -1))
        for copy in near:
            copy.wait()
        lax.fori_loop(0, 8, weigh, 0)
        all_of(got_ints, 8, int_ss, int_rs.at[1]).wait_recv()
        all_of(got_floats, 8, flo_ss, flo_rs.at[1]).wait_recv()
        far = to_scalars(1)
        take(1, range(7, -1, -1))

        @pl.when(get_edge)
        def _():
            all_of(got_edges, 16, edge_ss.at[0], edge_rs).wait_recv()
            for i in range(2):
                for d in range(16):
                    ff[16 * i + d, 0] = ff[16 * i + d, 0] + got_edges[d, i]

        zero = jnp.zeros((8, 128), F32)
        lax.fori_loop(0, 2, eight_modes, 0)
        for copy in far:
            copy.wait()
        parts = lax.fori_loop(0, 2, eight_far_modes, (zero, zero, zero))
        for n in range(16, MODES):
            parts = finish(n, got[n // 2, n % 2], parts)

        sum_a[...] = jnp.zeros((4, 128), F32)
        for i in range(3):
            sum_a[i : i + 1, :] = jnp.sum(parts[i], axis=0, keepdims=True)
        pl.semaphore_wait(here_sem, 16)
        for other in (0, 4):
            for f in FLIPS:
                a_copy(mode_of[f] + other, across).start()
                if other or f != SELF:
                    a_copy(mode_of[f] + other, s).start()
        sums_a[own_sum] = sum_a[...]
        all_of(sums_a, 15, a_ss, a_rs).wait_recv()

    @pl.when(sends)
    def _():
        all_of(sums_a, 16, a_ss, a_rs).wait_recv()

    def b_copy(d):
        return copy_to(sum_b, sums_b.at[z_at], b_ss, b_rs, along_z(d))

    def back_copy(f, other):
        src = img.at[pl.ds(2 * (r_of[f] + 2 * other), 2)]
        return copy_to(src, back.at[q], back_ss, back_rs, (mode_of[f] + other, s))

    sum_b[...] = jnp.sum(sums_a[...], axis=0)
    hear(2)
    for d in RING:
        b_copy(d).start()
    sums_b[z_at] = sum_b[...]

    @pl.when(works)
    def _():
        for f in FLIPS:
            back_copy(f, 4).start()
            if f != SELF:
                back_copy(f, 0).start()
        back[q] = img[pl.ds(2 * slot, 2)]
        all_of(back, 7, back_ss, back_rs).wait_recv()

    @pl.when(sends)
    def _():
        all_of(back, 8, back_ss, back_rs).wait_recv()

    for i in range(2):
        for z in range(2):
            for h in range(2):
                tile = pltpu.roll(back[4 * h, i], 7 - 4 * z, 0)
                for j in range(1, 4):
                    tile = jnp.where(sub // 2 == j, pltpu.roll(back[4 * h + j, i], (2 * j + 7 - 4 * z) % 8, 0), tile)
                image_ref[i, z, 8 * h : 8 * h + 8, :] = tile
    loads[5].wait()

    @pl.when(works)
    def _():
        all_of(pieces, 7, main_ss, main_rs.at[0]).wait_send()
        all_of(got_ints, 7, int_ss, int_rs.at[0]).wait_send()
        all_of(got_floats, 7, flo_ss, flo_rs.at[0]).wait_send()
        all_of(got, 15, back_ss, back_rs).wait_send()
        all_of(sums_b, 16, a_ss, a_rs).wait_send()
        all_of(sums_b, 15, a_ss, a_rs).wait_send()

    @pl.when(sends)
    def _():
        loads[4].wait()
        all_of(pieces, 8, main_ss, main_rs.at[0]).wait_send()
        all_of(got_ints, 8, int_ss, int_rs.at[0]).wait_send()
        all_of(got_floats, 8, flo_ss, flo_rs.at[0]).wait_send()

    @pl.when(put_kl)
    def _():
        kl_copy().wait_send()

    @pl.when(high)
    def _():
        edge_copy(1).wait_send()

    @pl.when(low)
    def _():
        edge_copy(0).wait_send()

    all_of(sums_b, 15, b_ss, b_rs).wait_recv()
    sums = jnp.sum(jnp.sum(sums_b[...], axis=0), axis=1, keepdims=True)
    norm, curve, energy = sums[0:1], sums[1:2], sums[2:3]
    step = curve / (energy + EPS)
    norm_new = jnp.maximum(norm - 2.0 * step * curve + step * step * energy, 0.0)
    beta = norm_new / (norm + EPS)
    for i in range(2):
        for z in range(2):
            for h in range(2):
                at = pl.ds(8 * h, 8)
                old = res[i, z, 8 + 8 * h : 16 + 8 * h, :]
                sol_ref[i, z, at, :] = sol[i, z, at, :] + step * old
                new = old - step * image_ref[i, z, at, :]
                res_ref[i, z, at, :] = new
                dir_ref[i, z, at, :] = new + beta * old
    all_of(sums_b, 15, b_ss, b_rs).wait_send()


def deliver(*refs):
    sem = refs[8]
    copies = [pltpu.make_async_copy(refs[i], refs[4 + i], sem.at[i]) for i in range(4)]
    for copy in copies:
        copy.start()
    for copy in copies:
        copy.wait()


def on_device(residual, solution, kl_terms, partner, kl_index, coefficient):
    vmem = pl.BlockSpec(memory_space=pltpu.VMEM)
    anywhere = pl.BlockSpec(memory_space=pl.ANY)
    dma = pltpu.SemaphoreType.DMA
    field = pltpu.VMEM(residual.shape, F32)
    i32 = jnp.int32
    results = pl.pallas_call(
        galerkin,
        out_shape=(field,) * 4,
        in_specs=[anywhere] * 6,
        out_specs=(vmem,) * 4,
        scratch_shapes=[
            pltpu.VMEM((2, 2, 32, 128), F32),
            pltpu.VMEM((2, 2, 16, 128), F32),
            pltpu.VMEM((KL, 2, 32, 128), F32),
            pltpu.VMEM((2, TERMS), i32),
            pltpu.VMEM((2, TERMS), i32),
            pltpu.VMEM((2, TERMS), F32),
            pltpu.VMEM((8, 2, 8, 128), F32),
            pltpu.VMEM((2, 2, 8, 128), F32),
            pltpu.VMEM((KL, 2, 128), F32),
            pltpu.VMEM((1, 128), i32),
            pltpu.VMEM((1, 128), F32),
            pltpu.VMEM((16, 2, 8, 128), F32),
            pltpu.VMEM((16, 2, 8, 128), F32),
            pltpu.VMEM((KL, 2, 128), F32),
            pltpu.VMEM((16, 1, 128), i32),
            pltpu.VMEM((16, 1, 128), F32),
            pltpu.SMEM((16, 1, 128), i32),
            pltpu.SMEM((16, 1, 128), F32),
            pltpu.VMEM((KL, 8, 128), F32),
            pltpu.VMEM((KL, 2, 8, 128), F32),
            pltpu.VMEM((MODES // 2, TERMS, 2, 8, 128), F32),
            pltpu.VMEM((MODES, 2, 8, 128), F32),
            pltpu.VMEM((MODES, 2, 8, 128), F32),
            pltpu.VMEM((MODES, 8, 128), F32),
            pltpu.VMEM((8, 2, 8, 128), F32),
            pltpu.VMEM((4, 128), F32),
            pltpu.VMEM((16, 4, 128), F32),
            pltpu.VMEM((4, 128), F32),
            pltpu.VMEM((16, 4, 128), F32),
            dma((6,)),
            dma, dma((16,)),
            dma((2,)), dma,
            dma, dma,
            dma, dma((2,)),
            dma, dma((2,)),
            dma((4,)),
            dma, dma,
            dma, dma,
            dma, dma,
            pltpu.SemaphoreType.REGULAR((3,)),
            pltpu.SemaphoreType.REGULAR,
        ],
        compiler_params=pltpu.CompilerParams(
            collective_id=0, has_side_effects=True, vmem_limit_bytes=60 << 20
        ),
        name="galerkin",
    )(residual, solution, kl_terms, partner, kl_index, coefficient)
    return pl.pallas_call(
        deliver,
        out_shape=(jax.ShapeDtypeStruct(residual.shape, F32),) * 4,
        in_specs=[vmem] * 4,
        out_specs=(anywhere,) * 4,
        scratch_shapes=[dma((4,))],
        compiler_params=pltpu.CompilerParams(vmem_limit_bytes=60 << 20),
        name="deliver",
    )(*(pltpu.with_memory_space_constraint(a, pltpu.VMEM) for a in results))


def solution(mesh):
    field = P("mode", None, "space", None)
    row = P("mode", None)
    return jax.shard_map(
        on_device,
        mesh=mesh,
        in_specs=(field, field, P(None, None, "space", None), row, row, row),
        out_specs=(field, field, field, field),
        check_vma=False,
    )
```
